128 devices in a mesh: rows: 128 (over y, x, z, core).
Axes of the slice: x: 4, y: 4, z: 4, core: 2. Of those that a mesh axis runs over, the one named last changes fastest.
Arguments:
- features: bfloat16 [16384, 256], P('rows'), may hold values from -6 to 6
- tile_values: bfloat16 [128, 16, 512, 512], P('rows'), may hold values from -0.0625 to 0.0625
- tile_col: int32 [128, 16], P('rows'), may hold values from 0 to 31, as said below
- tile_count: int32 [128], P('rows'), may hold values from 4 to 16, as said below
- weight: bfloat16 [256, 256], replicated, may hold values from -0.375 to 0.375
- bias: float32 [256], replicated, may hold values from -3 to 3
- cotangent: bfloat16 [65536, 256], P('rows'), may hold values from -6 to 6
Outputs:
- activation: bfloat16 [65536, 256], P('rows')
- grad_weight: float32 [256, 256], replicated
- grad_bias: float32 [256], replicated
- grad_features: float32 [16384, 256], P('rows')
The draws below stay inside these ranges and needn't reach their ends.
Inputs may be any that keep to these rules, and one draw needn't show every extreme that they name: `tile_count`: each row block uses between 4 and 16 slots, and some row block uses all 16. `tile_col`: the 16 tile columns of one row block are distinct.
All inputs are finite; a program needn't handle non-finite values.
Results may differ from the reference program's by a relative error of at most 0.011.
Values may be sent and summed in bfloat16 or wider, within the bound.
No kernel may reach another device: no remote copies, remote signals or barrier semaphores. Data moves between devices by JAX's collectives and lax.ppermute only.
A program may use at most 128 MiB of HBM per device.

```python
import jax
import jax.numpy as jnp
from jax import lax

H = 256
TILE = 512
NODES = 65536
COLS = 16384
CTILES = 32
SLOTS = 16
N_ROWS = 128


def draw_tile_count(key, part):
    key = jax.random.fold_in(key, 7)
    first, second = jax.random.split(key)
    counts = jax.random.randint(first, (N_ROWS,), SLOTS // 4, SLOTS + 1)
    where_full = jax.random.randint(second, (), 0, N_ROWS)
    places = jnp.arange(N_ROWS)
    return jnp.where(places == where_full, SLOTS, counts).astype(jnp.int32)


def row_order(row_key):
    return jax.random.permutation(row_key, CTILES)


def draw_tile_col(key, part):
    key = jax.random.fold_in(key, 11)
    row_keys = jax.random.split(key, N_ROWS)
    orders = jax.vmap(row_order)(row_keys).astype(jnp.int32)
    first = orders[0]
    top_col = CTILES - 1
    fixed = jnp.where(first == top_col, first[0], first)
    fixed = fixed.at[0].set(top_col)
    orders = orders.at[0].set(fixed)
    return orders[:, :SLOTS].astype(jnp.int32)


def level_of(own_key, dims, cuts, smallest, high):
    def one(axis_at, shards_of):
        heights = jax.random.uniform(jax.random.fold_in(jax.random.fold_in(own_key, 6), axis_at), (shards_of,), jnp.float32, smallest / len(cuts), high / len(cuts))
        return jnp.repeat(jnp.exp(heights), dims[axis_at] // shards_of).reshape((-1,) + (1,) * (len(dims) - axis_at - 1))

    factor_of = one(*cuts[0])
    for cut in cuts[1:]:
        factor_of = factor_of * one(*cut)
    return factor_of


def noise(key, shape, scale, bound, cuts=(), held_as=jnp.bfloat16):
    drawn = scale * jax.random.normal(key, shape, jnp.float32)
    if cuts:
        drawn = drawn * level_of(key, shape, cuts, -0.22, 0.18)
    return jnp.clip(drawn, -bound, bound).astype(held_as)


def setup_inputs(seed: int = 0) -> dict:
    seeds = jax.random.split(jax.random.key(seed), 8)
    features = noise(seeds[0], (COLS, H), 1.0, 6.0, ((0, 128),))
    tile_values = noise(seeds[1], (N_ROWS, SLOTS, TILE, TILE), (TILE * SLOTS) ** -0.5, 0.0625, ((0, 128),))
    tile_col = draw_tile_col(jax.random.fold_in(seeds[7], 71), 0)
    tile_count = draw_tile_count(jax.random.fold_in(seeds[7], 71), 0)
    weight = noise(seeds[4], (H, H), H ** -0.5, 0.375)
    bias = noise(seeds[5], (H,), 0.5, 3.0, (), jnp.float32)
    cotangent = noise(seeds[6], (NODES, H), 1.0, 6.0, ((0, 128),))
    return {"features": features, "tile_values": tile_values, "tile_col": tile_col, "tile_count": tile_count, "weight": weight, "bias": bias, "cotangent": cotangent}


def elu_grad(pre):
    return jnp.where(pre > 0, 1.0, jnp.exp(jnp.minimum(pre, 0.0)))

def reference(features, tile_values, tile_col, tile_count, weight, bias, cotangent):
    ctiles = COLS // TILE
    blocks = features.reshape(ctiles, TILE, H)
    slot_ids = jnp.arange(SLOTS, dtype=jnp.int32)

    def forward_block(item):
        values, cols, count = item
        live = (slot_ids < count).astype(jnp.float32)
        chosen = blocks[cols].astype(jnp.float32) * live[:, None, None]
        return jnp.einsum('sij,sjh->ih', values.astype(jnp.float32), chosen)
    agg = lax.map(forward_block, (tile_values, tile_col, tile_count))
    agg = agg.reshape(NODES, H).astype(jnp.bfloat16)
    pre = jnp.dot(agg, weight, preferred_element_type=jnp.float32) + bias
    activation = jax.nn.elu(pre).astype(jnp.bfloat16)
    grad_pre = (cotangent.astype(jnp.float32) * elu_grad(pre)).astype(jnp.bfloat16)
    scale = NODES ** (-0.5)
    grad_weight = jnp.dot(agg.T, grad_pre, preferred_element_type=jnp.float32) * scale
    grad_bias = lax.optimization_barrier(jnp.sum(grad_pre.astype(jnp.float32), axis=0)) * scale
    grad_rows = grad_pre.reshape(N_ROWS, TILE, H)
    col_ids = jnp.arange(ctiles, dtype=jnp.int32)

    def backward_block(carry, item):
        values, cols, count, local_grad = item
        live = (slot_ids < count).astype(jnp.float32)
        onehot = (cols[:, None] == col_ids[None, :]).astype(jnp.float32) * live[:, None]
        parts = jnp.einsum('sij,ih->sjh', values.astype(jnp.float32), local_grad.astype(jnp.float32))
        return (carry + jnp.einsum('sc,sjh->cjh', onehot, parts), None)
    start = jnp.zeros((ctiles, TILE, H), jnp.float32)
    back, unused = lax.scan(backward_block, start, (tile_values, tile_col, tile_count, grad_rows))
    back = back.reshape(COLS, H).astype(jnp.bfloat16)
    grad_features = lax.dot_general(back, weight, (((1,), (1,)), ((), ())), preferred_element_type=jnp.float32)
    return (activation, grad_weight, grad_bias, grad_features)
```

```python
import functools

import jax
import jax.numpy as jnp
import numpy as np
from jax import lax
from jax.experimental import pallas as pl
from jax.experimental.pallas import tpu as pltpu
from jax.sharding import PartitionSpec as P

AXIS = "rows"
SIZES = (4, 4, 4, 2)
Y, X, Z = 0, 1, 2
ORDERS = ((X, Y, Z), (Y, Z, X))
BF16 = jnp.bfloat16
F32 = jnp.float32
EXTRA = 272


def pairs(move):
    out = []
    for i in range(128):
        to = move([int(v) for v in np.unravel_index(i, SIZES)])
        to = [t % n for t, n in zip(to, SIZES)]
        out.append((i, int(np.ravel_multi_index(to, SIZES))))
    return out


def hop(x, phase, k):
    def move(at):
        at[ORDERS[at[3]][phase]] += k
        return at

    return lax.ppermute(x, AXIS, pairs(move))


def swap(x):
    def move(at):
        at[3] += 1
        return at

    return lax.ppermute(x, AXIS, pairs(move))


def dot(a, b, dims):
    return lax.dot_general(a, b, (dims, ((), ())), preferred_element_type=F32)


def split3(v):
    hi = v.astype(BF16)
    rest = v - hi.astype(F32)
    mid = rest.astype(BF16)
    low = (rest - mid.astype(F32)).astype(BF16)
    return hi, mid, low


def kernel(
    s_ref, a_hbm, mine, theirs, w_hbm, b_hbm, cot_hbm,
    act_hbm, rm_hbm, rt_hbm, em_hbm, et_hbm,
    a_buf, x_buf, acc, w_v, b_v, cot_v, act_v, g_t, out_buf, extra, zero, flags,
    sem_a, sem_x, sem_in, sem_o, sem_e, sem_act,
):
    count = s_ref[16]
    me = (s_ref[17], s_ref[18], s_ref[19])
    core = s_ref[20]

    def place(t, zlo, cc, sign):
        there = (lax.shift_right_logical(t, 3), lax.shift_right_logical(t, 1) & 3, (t & 1) * 2 + zlo)
        k = [((me[i] - there[i]) * sign) & 3 for i in range(3)]
        o = ORDERS[cc]
        return k[o[2]], k[o[1]] * 4 + k[o[0]]

    inputs = ((w_hbm, w_v), (b_hbm, b_v), (cot_hbm, cot_v))

    def load(s, carry):
        t = s_ref[s]
        for j in range(4):
            cc = j % 2
            k3, k21 = place(t, j // 2, cc, 1)
            to = x_buf.at[s, pl.ds(j * 128, 128)]

            @pl.when(core == cc)
            def _():
                pltpu.make_async_copy(mine.at[k3 * 16 + k21], to, sem_x.at[s, j]).start()

            @pl.when(core != cc)
            def _():
                pltpu.make_async_copy(theirs.at[k3 * 16 + k21], to, sem_x.at[s, j]).start()

        pltpu.make_async_copy(a_hbm.at[s], a_buf.at[s], sem_a.at[s]).start()
        return carry

    lax.fori_loop(0, count, load, 0)
    for i, (src, dst) in enumerate(inputs):
        pltpu.make_async_copy(src, dst, sem_in.at[i]).start()

    def send(src, t, j):
        cc = j % 2
        k3, k21 = place(t, j // 2, cc, -1)
        rows = pl.ds(k21 * 256, 256)

        @pl.when(core == cc)
        def _():
            pltpu.make_async_copy(src, rm_hbm.at[k3, rows], sem_o.at[t, j]).start()

        @pl.when(core != cc)
        def _():
            pltpu.make_async_copy(src, rt_hbm.at[k3, rows], sem_o.at[t, j]).start()

    zero[...] = jnp.zeros_like(zero)
    for t in range(32):
        flags[t] = 0

    def mark(s, carry):
        flags[s_ref[s]] = 1
        return carry

    lax.fori_loop(0, count, mark, 0)

    def clear(t, carry):
        @pl.when(flags[t] == 0)
        def _():
            for j in range(4):
                send(zero, t, j)

        return carry

    lax.fori_loop(0, 32, clear, 0)

    acc[...] = jnp.zeros_like(acc)

    def forward(s, carry):
        pltpu.make_async_copy(a_hbm.at[s], a_buf.at[s], sem_a.at[s]).wait()
        for j in range(4):
            to = x_buf.at[s, pl.ds(j * 128, 128)]
            pltpu.make_async_copy(mine.at[0], to, sem_x.at[s, j]).wait()
        acc[...] += dot(a_buf[s], x_buf[s], ((1,), (0,)))
        return carry

    lax.fori_loop(0, count, forward, 0)
    for i, (src, dst) in enumerate(inputs):
        pltpu.make_async_copy(src, dst, sem_in.at[i]).wait()

    agg = acc[...].astype(BF16)
    pre = dot(agg, w_v[...], ((1,), (0,))) + b_v[...]
    low = jnp.exp(jnp.minimum(pre, 0.0))
    act_v[...] = jnp.where(pre > 0, pre, low - 1.0).astype(BF16)
    act_copy = pltpu.make_async_copy(act_v, act_hbm, sem_act)
    act_copy.start()
    grad = (cot_v[...].astype(F32) * low).astype(BF16)
    g_t[...] = grad.astype(F32).T.astype(BF16)
    dw = dot(agg, grad, ((0,), (0,)))
    db = jnp.sum(grad.astype(F32), axis=0, keepdims=True)
    for h in range(2):
        half = slice(h * 128, h * 128 + 128)
        extra[h, :256, :] = dw[:, half].astype(BF16)
        row = lax.broadcasted_iota(jnp.int32, (16, 128), 0)
        hi, mid, low3 = [p.astype(F32) for p in split3(db[:, half])]
        parts = jnp.where(row == 0, hi, jnp.where(row == 1, mid, jnp.where(row == 2, low3, 0.0)))
        extra[h, 256:, :] = parts.astype(BF16)
    pltpu.make_async_copy(extra.at[core], em_hbm, sem_e.at[0]).start()
    pltpu.make_async_copy(extra.at[1 - core], et_hbm, sem_e.at[1]).start()

    def backward(s, carry):
        part = dot(g_t[...], a_buf[s], ((1,), (0,))).astype(BF16)
        for j in range(4):
            out_buf[s, j] = part[:, j * 128 : j * 128 + 128]
        for j in range(4):
            send(out_buf.at[s, j], s_ref[s], j)
        return carry

    lax.fori_loop(0, count, backward, 0)

    def finish(t, carry):
        for j in range(4):
            pltpu.make_async_copy(zero, rm_hbm.at[0, pl.ds(0, 256)], sem_o.at[t, j]).wait()
        return carry

    lax.fori_loop(0, 32, finish, 0)
    pltpu.make_async_copy(extra.at[0], em_hbm, sem_e.at[0]).wait()
    pltpu.make_async_copy(extra.at[1], et_hbm, sem_e.at[1]).wait()
    act_copy.wait()


def local(scalars, values, mine, theirs, weight, bias, cotangent):
    anywhere = pl.BlockSpec(memory_space=pl.ANY)
    return pl.pallas_call(
        kernel,
        out_shape=(
            jax.ShapeDtypeStruct((512, 256), BF16),
            jax.ShapeDtypeStruct((4, 4096, 128), BF16),
            jax.ShapeDtypeStruct((4, 4096, 128), BF16),
            jax.ShapeDtypeStruct((EXTRA, 128), BF16),
            jax.ShapeDtypeStruct((EXTRA, 128), BF16),
        ),
        in_specs=[pl.BlockSpec(memory_space=pltpu.SMEM)] + [anywhere] * 6,
        out_specs=(anywhere,) * 5,
        scratch_shapes=[
            pltpu.VMEM((16, 512, 512), BF16),
            pltpu.VMEM((16, 512, 256), BF16),
            pltpu.VMEM((512, 256), F32),
            pltpu.VMEM((256, 256), BF16),
            pltpu.VMEM((1, 256), F32),
            pltpu.VMEM((512, 256), BF16),
            pltpu.VMEM((512, 256), BF16),
            pltpu.VMEM((256, 512), BF16),
            pltpu.VMEM((16, 4, 256, 128), BF16),
            pltpu.VMEM((2, EXTRA, 128), BF16),
            pltpu.VMEM((256, 128), BF16),
            pltpu.SMEM((32,), jnp.int32),
            pltpu.SemaphoreType.DMA((16,)),
            pltpu.SemaphoreType.DMA((16, 4)),
            pltpu.SemaphoreType.DMA((3,)),
            pltpu.SemaphoreType.DMA((32, 4)),
            pltpu.SemaphoreType.DMA((2,)),
            pltpu.SemaphoreType.DMA,
        ],
        compiler_params=pltpu.CompilerParams(vmem_limit_bytes=28 * 1024 * 1024),
        cost_estimate=pl.CostEstimate(
            flops=2 * 2 * 16 * 512 * 512 * 256, bytes_accessed=32 * 2**20, transcendentals=512 * 256
        ),
        name="layer",
    )(scalars, values, mine, theirs, weight, bias, cotangent)


def add_up(parts):
    total = parts[0].astype(F32)
    for part in parts[1:]:
        total = total + part.astype(F32)
    return total


def exact_rows(total):
    db = total[256] + total[257] + total[258]
    hi = lax.reduce_precision(db, 8, 7)
    mid = lax.reduce_precision(db - hi, 8, 7)
    low = db - hi - mid
    row = lax.broadcasted_iota(jnp.int32, (16, 128), 0)
    bias = jnp.where(row == 0, hi, jnp.where(row == 1, mid, jnp.where(row == 2, low, 0.0)))
    return jnp.concatenate([total[:256], bias]).astype(BF16)


def on_device(features, tile_values, tile_col, tile_count, weight, bias, cotangent):
    me = lax.axis_index(AXIS)
    core = me & 1
    coords = jnp.stack([me >> 5, (me >> 3) & 3, (me >> 1) & 3, core]).astype(jnp.int32)
    scalars = jnp.concatenate([tile_col[0], tile_count, coords])

    held = features[None]
    for phase in range(2):
        held = jnp.concatenate([held] + [hop(held, phase, k) for k in (1, 2, 3)])
    got = [held] + [hop(held, 2, k) for k in (1, 2, 3)]
    mine = jnp.concatenate(got)
    theirs = jnp.concatenate([swap(g) for g in got])

    activation, r_mine, r_theirs, e_mine, e_theirs = local(
        scalars, tile_values[0], mine, theirs, weight, bias[None], cotangent
    )

    ride = exact_rows(add_up([e_mine, swap(e_theirs)]))
    terms = [None] * 4
    for k in (1, 3, 2, 0):
        body = add_up([r_mine[k], swap(r_theirs[k])]).astype(BF16)
        terms[k] = jnp.concatenate([body, ride])
    total = add_up([terms[0]] + [hop(terms[k], 2, k) for k in (1, 3, 2)])
    for phase in (1, 0):
        ride = exact_rows(total[-EXTRA:])
        rows = (total.shape[0] - EXTRA) // 4
        body = total[:-EXTRA].astype(BF16)
        terms = [jnp.concatenate([body[k * rows : k * rows + rows], ride]) for k in range(4)]
        total = add_up([terms[0]] + [hop(terms[k], phase, k) for k in (1, 3, 2)])
    back = total[:256].astype(BF16)
    grad_features = dot(back, weight, ((0,), (1,)))

    scale = 65536 ** (-0.5)
    own = total[256:]
    own_dw = own[:256] * scale
    own_db = ((own[256] + own[257]) + own[258]) * scale
    own = jnp.concatenate([own_dw, jnp.broadcast_to(own_db, (8, 128))])
    other = swap(own)
    first = jnp.where(core == 0, own, other)
    second = jnp.where(core == 0, other, own)
    both = jnp.concatenate([first, second], axis=1)
    return activation, both[:256], both[256], grad_features


def solution(mesh):
    in_specs = (
        P("rows", None),
        P("rows", None, None, None),
        P("rows", None),
        P("rows"),
        P(),
        P(),
        P("rows", None),
    )
    out_specs = (P("rows", None), P(), P(), P("rows", None))
    return jax.shard_map(
        on_device, mesh=mesh, in_specs=in_specs, out_specs=out_specs, check_vma=False
    )
```

```python
import functools

import jax
import jax.numpy as jnp
import numpy as np
from jax import lax
from jax.experimental import pallas as pl
from jax.experimental.pallas import tpu as pltpu
from jax.sharding import PartitionSpec as P

AXIS = "rows"
SIZES = (4, 4, 4, 2)
Y, X, Z = 0, 1, 2
ORDERS = ((X, Y, Z), (Y, Z, X))
BF16 = jnp.bfloat16
F32 = jnp.float32
GROUP = 8
STARTS = (0, 8, 16, 56, 24, 48, 32, 40)
EXTRA = 272


def pairs(move):
    out = []
    for i in range(128):
        to = move([int(v) for v in np.unravel_index(i, SIZES)])
        to = [t % n for t, n in zip(to, SIZES)]
        out.append((i, int(np.ravel_multi_index(to, SIZES))))
    return out


def hop(x, phase, k):
    def move(at):
        at[ORDERS[at[3]][phase]] += k
        return at

    return lax.ppermute(x, AXIS, pairs(move))


def swap(x):
    def move(at):
        at[3] += 1
        return at

    return lax.ppermute(x, AXIS, pairs(move))


def dot(a, b, dims):
    return lax.dot_general(a, b, (dims, ((), ())), preferred_element_type=F32)


def cut_in_kernel(v):
    return v.astype(BF16).astype(F32)


def cut(v):
    return lax.reduce_precision(v, 8, 7)


def split3(v, cut):
    hi = cut(v)
    mid = cut(v - hi)
    return hi, mid, (v - hi) - mid


def load_kernel(a_hbm, a_ref, sem):
    copies = [
        pltpu.make_async_copy(a_hbm.at[s], a_ref.at[:, pl.ds(s * 512, 512)], sem.at[s])
        for s in range(16)
    ]
    for copy in copies:
        copy.start()
    for copy in copies:
        copy.wait()


def load(values):
    return pl.pallas_call(
        load_kernel,
        out_shape=pltpu.VMEM((512, 8192), BF16),
        in_specs=[pl.BlockSpec(memory_space=pltpu.HBM)],
        out_specs=pl.BlockSpec(memory_space=pltpu.VMEM),
        scratch_shapes=[pltpu.SemaphoreType.DMA((16,))],
        compiler_params=pltpu.CompilerParams(vmem_limit_bytes=1024 * 1024),
        cost_estimate=pl.CostEstimate(flops=0, bytes_accessed=2 * 8 * 2**20, transcendentals=0),
        name="load",
    )(pltpu.with_memory_space_constraint(values, pltpu.HBM))


def kernel(
    col_ref, count_ref, a_ref, w_ref, b_ref, cot_ref, *rest,
):
    blocks, (act_ref, r_ref, e_ref, g_buf, x_buf, acc, g_t) = rest[:16], rest[16:]
    count = count_ref[0]
    index = lax.axis_index(AXIS)
    me = (index >> 5, (index >> 3) & 3, (index >> 1) & 3)
    core = index & 1

    def place(t, zlo, cc, sign):
        there = (lax.shift_right_logical(t, 3), lax.shift_right_logical(t, 1) & 3, (t & 1) * 2 + zlo)
        k = [((me[i] - there[i]) * sign) & 3 for i in range(3)]
        o = ORDERS[cc]
        return k[o[2]], k[o[1]] * 4 + k[o[0]]

    for side in range(2):
        for ref, start in zip(blocks[side * 8 : side * 8 + 8], STARTS):
            g_buf[side, start : start + ref.shape[0]] = ref[...]
    r_ref[...] = jnp.zeros_like(r_ref)
    acc[...] = jnp.zeros_like(acc)

    def forward(g, carry):
        for q in range(GROUP):
            s = g * GROUP + q
            t = col_ref[0, s]
            live = s < count
            for j in range(4):
                cc = j % 2
                k3, k21 = place(t, j // 2, cc, 1)
                at = k3 * 16 + k21
                piece = g_buf[jnp.where(core == cc, 0, 1), at]
                rows = slice(q * 512 + j * 128, q * 512 + j * 128 + 128)
                x_buf[rows] = jnp.where(live, piece, jnp.zeros_like(piece))
        columns = pl.ds(pl.multiple_of(g * (GROUP * 512), GROUP * 512), GROUP * 512)
        acc[...] += dot(a_ref[:, columns], x_buf[...], ((1,), (0,)))
        return carry

    lax.fori_loop(0, 16 // GROUP, forward, 0)

    agg = acc[...].astype(BF16)
    pre = dot(agg, w_ref[...], ((1,), (0,))) + b_ref[...]
    low = jnp.exp(jnp.minimum(pre, 0.0))
    act_ref[...] = jnp.where(pre > 0, pre, low - 1.0).astype(BF16)
    grad = (cot_ref[...].astype(F32) * low).astype(BF16)
    g_t[...] = grad.astype(F32).T.astype(BF16)
    dw = dot(agg, grad, ((0,), (0,)))
    db = jnp.sum(grad.astype(F32), axis=0, keepdims=True)
    for h in range(2):
        half = slice(h * 128, h * 128 + 128)
        side = jnp.where(core == h, 0, 1)
        e_ref[side, :256, :] = dw[:, half].astype(BF16)
        row = lax.broadcasted_iota(jnp.int32, (16, 128), 0)
        hi, mid, low3 = split3(db[:, half], cut_in_kernel)
        parts = jnp.where(row == 0, hi, jnp.where(row == 1, mid, jnp.where(row == 2, low3, 0.0)))
        e_ref[side, 256:, :] = parts.astype(BF16)

    def backward(g, carry):
        for q in range(GROUP):
            s = g * GROUP + q
            t = col_ref[0, s]
            columns = pl.ds(pl.multiple_of(s * 512, 512), 512)
            part = dot(g_t[...], a_ref[:, columns], ((1,), (0,)))
            part = jnp.where(s < count, part, 0.0).astype(BF16)
            for j in range(4):
                cc = j % 2
                k3, k21 = place(t, j // 2, cc, -1)
                side = jnp.where(core == cc, 0, 1)
                rows = pl.ds(pl.multiple_of(k21 * 256, 256), 256)
                r_ref[side * 4 + k3, rows] = part[:, j * 128 : j * 128 + 128]
        return carry

    lax.fori_loop(0, 16 // GROUP, backward, 0)


def local(cols, count, values, weight, bias, cotangent, blocks):
    vmem = pl.BlockSpec(memory_space=pltpu.VMEM)
    return pl.pallas_call(
        kernel,
        out_shape=(
            pltpu.VMEM((512, 256), BF16),
            pltpu.VMEM((8, 4096, 128), BF16),
            pltpu.VMEM((2, EXTRA, 128), BF16),
        ),
        in_specs=[pl.BlockSpec(memory_space=pltpu.SMEM)] * 2 + [vmem] * 20,
        out_specs=(vmem,) * 3,
        scratch_shapes=[
            pltpu.VMEM((2, 64, 128, 256), BF16),
            pltpu.VMEM((GROUP * 512, 256), BF16),
            pltpu.VMEM((512, 256), F32),
            pltpu.VMEM((256, 512), BF16),
        ],
        compiler_params=pltpu.CompilerParams(vmem_limit_bytes=18 * 1024 * 1024),
        cost_estimate=pl.CostEstimate(
            flops=2 * 2 * 16 * 512 * 512 * 256, bytes_accessed=8 * 2**20, transcendentals=512 * 256
        ),
        name="layer",
    )(cols, count, values, weight, bias, cotangent, *blocks)


def in_vmem(name, body, outs, *ins):
    vmem = pl.BlockSpec(memory_space=pltpu.VMEM)
    size = sum(int(np.prod(o.shape)) * 2 for o in (*outs, *ins))
    return pl.pallas_call(
        body,
        out_shape=tuple(pltpu.VMEM(o.shape, o.dtype) for o in outs),
        in_specs=[vmem] * len(ins),
        out_specs=(vmem,) * len(outs),
        compiler_params=pltpu.CompilerParams(vmem_limit_bytes=4 * 1024 * 1024),
        cost_estimate=pl.CostEstimate(flops=0, bytes_accessed=size // 4, transcendentals=0),
        name=name,
    )(*ins)


def like(*shape):
    return jax.ShapeDtypeStruct(shape, BF16)


def join(parts, pieces=1):
    rows = sum(p.shape[0] for p in parts) // pieces

    def body(*refs):
        at = 0
        for ref in refs[: len(parts)]:
            for i in range(ref.shape[0]):
                refs[len(parts) + at // rows][at % rows] = ref[i]
                at += 1

    outs = [like(rows, *parts[0].shape[1:])] * pieces
    return in_vmem("join", body, outs, *parts)


def add_up(parts):
    total = parts[0].astype(F32)
    for part in parts[1:]:
        total = total + part.astype(F32)
    return total


def widened(*refs):
    total = refs[0].astype(F32)
    for ref in refs[1:]:
        total = total + ref.astype(F32)
    return total


def exact_rows(total, cut):
    db = total[256:257] + total[257:258] + total[258:259]
    row = lax.broadcasted_iota(jnp.int32, (16, 128), 0)
    hi, mid, low = split3(db, cut)
    bias = jnp.where(row == 0, hi, jnp.where(row == 1, mid, jnp.where(row == 2, low, 0.0)))
    return total[:256].astype(BF16), bias.astype(BF16)


def put_extra(ref, at, total):
    top, bias = exact_rows(total, cut_in_kernel)
    ref[at : at + 256] = top
    ref[at + 256 : at + EXTRA] = bias


def first_terms(a, b, ea, eb, o1, o2, ride):
    put_extra(ride, 0, widened(ea[...], eb[...]))
    o1[:2048] = widened(a[:2048], b[:2048]).astype(BF16)
    o2[:2048] = widened(a[2048:], b[2048:]).astype(BF16)
    o1[2048:] = ride[...]
    o2[2048:] = ride[...]


def direct_terms(a, b, o):
    o[...] = widened(a[...], b[...]).astype(BF16)


def passed_terms(a, b, got, o):
    o[:2048] = widened(a[...], b[...], got[:2048]).astype(BF16)
    if o.shape[0] > 2048:
        o[2048:] = got[2048:]


def on_device(features, tile_values, tile_col, tile_count, weight, bias, cotangent):
    core = lax.axis_index(AXIS) & 1

    values = load(tile_values[0])
    held = features[None]
    held = join([held] + [hop(held, 0, k) for k in (1, 2, 3)])[0]
    held, values = lax.optimization_barrier((held, values))
    h1, h2 = join([held] + [hop(held, 1, k) for k in (1, 2, 3)], 2)
    a1, b2 = hop(h1, 2, 1), hop(h2, 2, 3)
    a2, b1 = hop(h2, 2, 1), hop(h1, 2, 3)
    c1, c2 = hop(a1, 2, 1), hop(b2, 2, 3)
    mine = [h1, h2, a1, b2, a2, b1, c1, c2]
    theirs = [swap(g) for g in mine]

    activation, r_all, e_all = local(
        tile_col, tile_count, values, weight, bias[None], cotangent, mine + theirs
    )

    o1, o2, ride = in_vmem(
        "first_terms", first_terms, [like(2048 + EXTRA, 128)] * 2 + [like(EXTRA, 128)],
        r_all[2], swap(r_all[6]), e_all[0], swap(e_all[1]),
    )
    o1, o2, r_all = lax.optimization_barrier((o1, o2, r_all))
    via1, via3 = hop(o1, 2, 1), hop(o2, 2, 3)
    t1, t3 = swap(r_all[5]), swap(r_all[7])
    half = [like(2048, 128)]
    d1 = in_vmem("direct_terms", direct_terms, half, r_all[1, 2048:], t1[2048:])[0]
    d3 = in_vmem("direct_terms", direct_terms, half, r_all[3, :2048], t3[:2048])[0]
    d1, d3 = hop(d1, 2, 1), hop(d3, 2, 3)
    t0 = swap(r_all[4])
    p1 = in_vmem("passed_terms", passed_terms, [like(2048 + EXTRA, 128)], r_all[1, :2048], t1[:2048], via1)[0]
    p3 = in_vmem("passed_terms", passed_terms, half, r_all[3, 2048:], t3[2048:], via3[:2048])[0]
    p1, p3 = hop(p1, 2, 1), hop(p3, 2, 3)

    total = jnp.concatenate([
        add_up([r_all[0, :2048], t0[:2048], d3, p1[:2048]]),
        add_up([r_all[0, 2048:], t0[2048:], d1, p3]),
        add_up([ride, via1[2048:], via3[2048:], p1[2048:]]),
    ])
    for phase in (1, 0):
        ride = jnp.concatenate(exact_rows(total[-EXTRA:], cut))
        rows = (total.shape[0] - EXTRA) // 4
        body = total[:-EXTRA].astype(BF16)
        terms = [jnp.concatenate([body[k * rows : k * rows + rows], ride]) for k in range(4)]
        own = jnp.concatenate([total[:rows], total[-EXTRA:]])
        total = add_up([own] + [hop(terms[k], phase, k) for k in (1, 3, 2)])
    back = total[:256].astype(BF16)
    grad_features = dot(back, weight, ((0,), (1,)))

    scale = 65536 ** (-0.5)
    own = total[256:]
    own_dw = own[:256] * scale
    own_db = ((own[256] + own[257]) + own[258]) * scale
    own = jnp.concatenate([own_dw, jnp.broadcast_to(own_db, (8, 128))])
    other = swap(own)
    first = jnp.where(core == 0, own, other)
    second = jnp.where(core == 0, other, own)
    both = jnp.concatenate([first, second], axis=1)
    return activation, both[:256], both[256], grad_features


def solution(mesh):
    in_specs = (
        P("rows", None),
        P("rows", None, None, None),
        P("rows", None),
        P("rows"),
        P(),
        P(),
        P("rows", None),
    )
    out_specs = (P("rows", None), P(), P(), P("rows", None))
    return jax.shard_map(
        on_device, mesh=mesh, in_specs=in_specs, out_specs=out_specs, check_vma=False
    )
```

```python
import functools

import jax
import jax.numpy as jnp
import numpy as np
from jax import lax
from jax.experimental import pallas as pl
from jax.experimental.pallas import tpu as pltpu
from jax.sharding import PartitionSpec as P

AXIS = "rows"
SIZES = (4, 4, 4, 2)
Y, X, Z = 0, 1, 2
PLANES = ((Y, Z), (Y, X))
LINE = (X, Z)
STEPS = ((Y, Z), (X, Y))
BF16 = jnp.bfloat16
F32 = jnp.float32
GROUP = 8
STARTS = ((0,), (16, 56), (24, 48), (32,), (40,))
DB = 16


def device(at):
    return int(np.ravel_multi_index([t % n for t, n in zip(at, SIZES)], SIZES))


def groups(axes):
    out = {}
    for i in range(128):
        at = [int(v) for v in np.unravel_index(i, SIZES)]
        own = axes[at[3]]
        key = tuple(-1 if a in own else at[a] for a in range(4))
        out.setdefault(key, []).append((tuple(at[a] for a in own), i))
    return [[i for _, i in sorted(members)] for _, members in sorted(out.items())]


def exchange(x, axes):
    return lax.all_to_all(
        x, AXIS, split_axis=0, concat_axis=0, tiled=True, axis_index_groups=groups(axes)
    )


def pairs(move):
    return [(i, device(move([int(v) for v in np.unravel_index(i, SIZES)]))) for i in range(128)]


def hop(x, axes, k):
    def move(at):
        at[axes[at[3]]] += k
        return at

    return lax.ppermute(x, AXIS, pairs(move))


def around(x, axes):
    return [hop(x, axes, k) for k in (3, 2, 1)]


def swap(x):
    def move(at):
        at[3] += 1
        return at

    return lax.ppermute(x, AXIS, pairs(move))


def dot(a, b, dims):
    return lax.dot_general(a, b, (dims, ((), ())), preferred_element_type=F32)


def load_kernel(a_hbm, a_ref, sem):
    copies = [
        pltpu.make_async_copy(a_hbm.at[s], a_ref.at[:, pl.ds(s * 512, 512)], sem.at[s])
        for s in range(16)
    ]
    for copy in copies:
        copy.start()
    for copy in copies:
        copy.wait()


def load(values):
    return pl.pallas_call(
        load_kernel,
        out_shape=pltpu.VMEM((512, 8192), BF16),
        in_specs=[pl.BlockSpec(memory_space=pltpu.HBM)],
        out_specs=pl.BlockSpec(memory_space=pltpu.VMEM),
        scratch_shapes=[pltpu.SemaphoreType.DMA((16,))],
        compiler_params=pltpu.CompilerParams(vmem_limit_bytes=1024 * 1024),
        cost_estimate=pl.CostEstimate(flops=0, bytes_accessed=2 * 8 * 2**20, transcendentals=0),
        name="load",
    )(pltpu.with_memory_space_constraint(values, pltpu.HBM))


def kernel(
    col_ref, count_ref, a_ref, w_ref, b_ref, cot_ref, *rest,
):
    blocks, (act_ref, r_ref, e_ref, g_buf, x_buf, acc, g_t) = rest[:10], rest[10:]
    count = count_ref[0]
    index = lax.axis_index(AXIS)
    me = (index >> 5, (index >> 3) & 3, (index >> 1) & 3)
    core = index & 1

    def there(t, zlo):
        return lax.shift_right_logical(t, 3), lax.shift_right_logical(t, 1) & 3, (t & 1) * 2 + zlo

    def source(t, zlo, cc):
        at = there(t, zlo)
        away = [(at[i] - me[i]) & 3 for i in range(3)]
        first, second = STEPS[cc]
        return (-away[LINE[cc]] & 3) * 16 + away[second] * 4 + away[first]

    def target(t, zlo, cc):
        at = there(t, zlo)
        away = [(at[i] - me[i]) & 3 for i in range(3)]
        first, second = STEPS[cc]
        return away[LINE[cc]], away[second] * 4 + away[first]

    for side in range(2):
        for ref, starts in zip(blocks[side * 5 : side * 5 + 5], STARTS):
            length = ref.shape[0] // len(starts)
            for i, start in enumerate(starts):
                g_buf[side, start : start + length] = ref[i * length : i * length + length]
    r_ref[...] = jnp.zeros_like(r_ref)
    acc[...] = jnp.zeros_like(acc)

    def forward(g, carry):
        for q in range(GROUP):
            s = g * GROUP + q
            t = col_ref[0, s]
            live = s < count
            for j in range(4):
                cc = j % 2
                at = source(t, j // 2, cc)
                piece = g_buf[jnp.where(core == cc, 0, 1), at]
                rows = slice(q * 512 + j * 128, q * 512 + j * 128 + 128)
                x_buf[rows] = jnp.where(live, piece, jnp.zeros_like(piece))
        columns = pl.ds(pl.multiple_of(g * (GROUP * 512), GROUP * 512), GROUP * 512)
        acc[...] += dot(a_ref[:, columns], x_buf[...], ((1,), (0,)))
        return carry

    lax.fori_loop(0, 16 // GROUP, forward, 0)

    agg = acc[...].astype(BF16)
    pre = dot(agg, w_ref[...], ((1,), (0,))) + b_ref[...]
    low = jnp.exp(jnp.minimum(pre, 0.0))
    act_ref[...] = jnp.where(pre > 0, pre, low - 1.0).astype(BF16)
    grad = (cot_ref[...].astype(F32) * low).astype(BF16)
    g_t[...] = grad.astype(F32).T.astype(BF16)
    dw = dot(agg, grad, ((0,), (0,)))
    db = jnp.sum(grad.astype(F32), axis=0, keepdims=True)
    for h in range(2):
        half = slice(h * 128, h * 128 + 128)
        side = jnp.where(core == h, 0, 1)
        e_ref[side, :256] = dw[:, half]
        e_ref[side, 256:] = jnp.broadcast_to(db[:, half], (8, 128))

    def backward(g, carry):
        for q in range(GROUP):
            s = g * GROUP + q
            t = col_ref[0, s]
            columns = pl.ds(pl.multiple_of(s * 512, 512), 512)
            part = dot(g_t[...], a_ref[:, columns], ((1,), (0,)))
            part = jnp.where(s < count, part, 0.0).astype(BF16)
            for j in range(4):
                cc = j % 2
                k3, k21 = target(t, j // 2, cc)
                rows = pl.ds(pl.multiple_of(k21 * 256, 256), 256)
                other = jnp.where(k3 == 0, 7, jnp.where(k3 == 1, 5, jnp.where(k3 == 2, 4, 6)))
                r_ref[jnp.where(core == cc, k3, other), rows] = part[:, j * 128 : j * 128 + 128]
        return carry

    lax.fori_loop(0, 16 // GROUP, backward, 0)


def local(cols, count, values, weight, bias, cotangent, blocks):
    vmem = pl.BlockSpec(memory_space=pltpu.VMEM)
    return pl.pallas_call(
        kernel,
        out_shape=(
            pltpu.VMEM((512, 256), BF16),
            pltpu.VMEM((8, 4096, 128), BF16),
            pltpu.VMEM((2, 264, 128), F32),
        ),
        in_specs=[pl.BlockSpec(memory_space=pltpu.SMEM)] * 2 + [vmem] * 14,
        out_specs=(vmem,) * 3,
        scratch_shapes=[
            pltpu.VMEM((2, 64, 128, 256), BF16),
            pltpu.VMEM((GROUP * 512, 256), BF16),
            pltpu.VMEM((512, 256), F32),
            pltpu.VMEM((256, 512), BF16),
        ],
        compiler_params=pltpu.CompilerParams(vmem_limit_bytes=18 * 1024 * 1024),
        cost_estimate=pl.CostEstimate(
            flops=2 * 2 * 16 * 512 * 512 * 256, bytes_accessed=8 * 2**20, transcendentals=512 * 256
        ),
        name="layer",
    )(cols, count, values, weight, bias, cotangent, *blocks)


def in_vmem(name, body, outs, *ins, last=False):
    vmem = pl.BlockSpec(memory_space=pltpu.VMEM)
    size = sum(int(np.prod(o.shape)) * 2 for o in (*outs, *ins))
    return pl.pallas_call(
        body,
        out_shape=tuple(o if last else pltpu.VMEM(o.shape, o.dtype) for o in outs),
        in_specs=[vmem] * len(ins),
        out_specs=(vmem,) * len(outs),
        compiler_params=pltpu.CompilerParams(vmem_limit_bytes=4 * 1024 * 1024),
        cost_estimate=pl.CostEstimate(flops=0, bytes_accessed=size // 4, transcendentals=0),
        name=name,
    )(*ins)


def like(*shape, dtype=BF16):
    return jax.ShapeDtypeStruct(shape, dtype)


def widened(*parts):
    total = parts[0].astype(F32)
    for part in parts[1:]:
        total = total + part.astype(F32)
    return total


def join(*parts):
    def body(*refs):
        at = 0
        for ref in refs[:-1]:
            refs[-1][at : at + ref.shape[0]] = ref[...]
            at += ref.shape[0]

    rows = sum(p.shape[0] for p in parts)
    return in_vmem("join", body, [like(rows, *parts[0].shape[1:])], *parts)[0]


def halves(x, lower, upper):
    lower[...] = x[:8]
    upper[...] = x[8:]


def add_rows(o, start, *parts):
    o[start : start + 256] = widened(*[ref[at : at + 256] for ref, at in parts]).astype(BF16)


def split(v):
    hi = v.astype(BF16).astype(F32)
    return hi, v - hi


def first_terms(r, t, e, te, o1, o3, ride):
    total = e[0] + te[...]
    hi, low = split(total[256:])
    ride[:256] = total[:256].astype(BF16)
    ride[256:] = jnp.concatenate([hi, low]).astype(BF16)
    for at in range(0, 2048, 256):
        add_rows(o1, at, (r.at[2], at), (t, at))
        add_rows(o3, at, (r.at[2], at + 2048), (t, at + 2048))
    o1[2048:] = ride[...]
    o3[2048:] = ride[...]


def extra_pieces(e, te, via1, via3, far, o):
    total = e[0] + te[...]
    dw = total[:256] + widened(via1[2048:2304], via3[2048:2304], far[:256])
    db = total[256:] + widened(via1[2304:2312], via1[2312:], via3[2304:2312], via3[2312:], far[256:264], far[264:])
    for i in range(16):
        o[i, :DB] = dw[i * 16 : i * 16 + 16]
        o[i, DB:] = db


def second_terms(r, t, via1, via3, _pieces, p1, p3):
    for at in range(0, 2048, 256):
        up = at + 2048
        add_rows(p1, at, (r.at[1], at), (t.at[0], at), (via1, at))
        add_rows(p1, up, (r.at[1], up), (t.at[0], up))
        add_rows(p3, at, (r.at[3], at), (t.at[1], at))
        add_rows(p3, up, (r.at[3], up), (t.at[1], up), (via3, at))


def line_sum(r, t0, p1, p3, got, own, piece, m1, m2, m3):
    total = got[0]
    for i in range(1, 16):
        total = total + got[i]
    total = total * 65536 ** (-0.5)
    hi, low = split(total[DB:])
    piece[...] = jnp.concatenate([total[:DB], hi, low]).astype(BF16)
    for k, message in enumerate((None, m1, m2, m3)):
        for at in range(0, 1024, 256):
            rows = slice(k * 1024 + at, k * 1024 + at + 256)
            terms = widened(r[0, rows], t0[rows], p1[rows], p3[rows])
            if message is None:
                own[at : at + 256] = terms
            else:
                message[at : at + 256] = terms.astype(BF16)
        if message is not None:
            message[1024:] = piece[...]


def plane_sum(own, piece, g1, g2, g3, rest, pieces, n1, n2, n3):
    for i, ref in enumerate((piece, g1, g2, g3)):
        pieces[i * 32 : i * 32 + 32] = ref[-32:]
    for k, message in enumerate((None, n1, n2, n3)):
        rows = slice(k * 256, k * 256 + 256)
        terms = own[rows] + widened(g1[rows], g2[rows], g3[rows])
        if message is None:
            rest[...] = terms
        else:
            message[:256] = terms.astype(BF16)
            message[256:] = pieces[...]


def extra_half(pieces, h1, h2, h3, o):
    index = lax.axis_index(AXIS)
    at = (index >> 5, (index >> 3) & 3, (index >> 1) & 3)

    def choose(axes):
        return jnp.where((index & 1) == 0, at[axes[0]], at[axes[1]])

    first, second = (choose(axes) for axes in zip(*STEPS))
    flip = [STEPS[c] != PLANES[c] for c in range(2)]
    flip = jnp.where((index & 1) == 0, int(flip[0]), int(flip[1])) == 1
    for k1, (ref, base) in enumerate(((pieces, 0), (h1, 256), (h2, 256), (h3, 256))):
        for k2 in range(4):
            i, j = (first - k1) & 3, (second - k2) & 3
            place = jnp.where(flip, j * 4 + i, i * 4 + j)
            start = base + k2 * 32
            o[pl.ds(pl.multiple_of(place * 16, 16), 16)] = ref[start : start + DB].astype(F32)
    o[256:] = widened(pieces[DB : DB + 8], pieces[DB + 8 : DB + 16])


def extra_both(core, own, other, dw, db):
    here = core == 0
    first = jnp.where(here, own[...], other[...])
    second = jnp.where(here, other[...], own[...])
    dw[:, :128], dw[:, 128:] = first[:256], second[:256]
    db[:, :128], db[:, 128:] = first[256:257], second[256:257]


def finish(rest, h1, h2, h3, w, o):
    total = rest[...] + widened(h1[:256], h2[:256], h3[:256])
    o[...] = dot(total.T.astype(BF16), w[...], ((1,), (1,)))


def keep(x_ref, o_ref, sem):
    copy = pltpu.make_async_copy(x_ref, o_ref, sem)
    copy.start()
    copy.wait()


def to_output(x):
    return pl.pallas_call(
        keep,
        out_shape=like(*x.shape),
        in_specs=[pl.BlockSpec(memory_space=pltpu.VMEM)],
        out_specs=pl.BlockSpec(memory_space=pltpu.HBM),
        scratch_shapes=[pltpu.SemaphoreType.DMA],
        compiler_params=pltpu.CompilerParams(vmem_limit_bytes=1024 * 1024),
        name="to_output",
    )(x)


def on_device(features, tile_values, tile_col, tile_count, weight, bias, cotangent):
    values = load(tile_values[0])
    held = features[None]
    first, second = zip(*STEPS)
    held = join(held, *around(held, first))
    held, values = lax.optimization_barrier((held, values))
    held = join(held, *around(held, second))
    h1, h2 = in_vmem("halves", halves, [like(8, 128, 256)] * 2, held)
    a1, b2, a2, b1 = hop(h1, LINE, 1), hop(h2, LINE, 3), hop(h2, LINE, 1), hop(h1, LINE, 3)
    a1, b2, other = lax.optimization_barrier((a1, b2, held))
    c1, c2 = hop(a1, LINE, 1), hop(b2, LINE, 3)
    mine = [held, join(a1, b2), join(a2, b1), c1, c2]
    theirs = [swap(other)] + [swap(g) for g in mine[1:]]
    activation, r_all, e_all = local(
        tile_col, tile_count, values, weight, bias[None], cotangent, mine + theirs
    )

    some, whole = like(2048 + 272, 128), like(4096, 128)
    e_theirs = swap(e_all[1])
    o1, o3, ride = in_vmem(
        "first_terms", first_terms, [some, some, like(272, 128)],
        r_all, swap(r_all[4]), e_all, e_theirs,
    )
    o1, o3, ride, beside, activation = lax.optimization_barrier(
        (o1, o3, ride, r_all[5:7], activation)
    )
    via1, via3, far = hop(o1, LINE, 1), hop(o3, LINE, 3), hop(ride, LINE, 2)
    beside = swap(beside)
    activation = to_output(activation)
    pieces = in_vmem(
        "extra_pieces", extra_pieces, [like(16, 24, 128, dtype=F32)],
        e_all, e_theirs, via1, via3, far,
    )[0]
    p1, p3 = in_vmem(
        "second_terms", second_terms, [whole, whole], r_all, beside, via1, via3, pieces
    )
    p1, p3, pieces, activation, own = lax.optimization_barrier(
        (p1, p3, pieces, activation, r_all[7])
    )
    p1, p3 = hop(p1, LINE, 1), hop(p3, LINE, 3)
    pieces = exchange(pieces, PLANES)
    own, piece, *sent = in_vmem(
        "line_sum", line_sum, [like(1024, 128, dtype=F32), like(32, 128)] + [like(1056, 128)] * 3,
        r_all, swap(own), p1, p3, pieces,
    )
    got = [hop(m, second, k) for k, m in zip((1, 2, 3), sent)]
    rest, pieces, *sent = in_vmem(
        "plane_sum", plane_sum, [like(256, 128, dtype=F32), like(128, 128)] + [like(384, 128)] * 3,
        own, piece, *got,
    )
    got = [hop(m, first, k) for k, m in zip((1, 2, 3), sent)]
    own = in_vmem("extra_half", extra_half, [like(264, 128, dtype=F32)], pieces, *got)[0]
    other = swap(own)
    grad_features = in_vmem(
        "finish", finish, [like(128, 256, dtype=F32)], rest, *got, weight, last=True
    )[0]
    grad_weight, grad_bias = extras(own, other)
    return activation, grad_weight, grad_bias[0], grad_features


def extras(own, other):
    vmem = pl.BlockSpec(memory_space=pltpu.VMEM)

    def body(own, other, dw, db):
        extra_both(lax.axis_index(AXIS) & 1, own, other, dw, db)

    return pl.pallas_call(
        body,
        out_shape=(like(256, 256, dtype=F32), like(1, 256, dtype=F32)),
        in_specs=[vmem] * 2,
        out_specs=(vmem,) * 2,
        compiler_params=pltpu.CompilerParams(vmem_limit_bytes=4 * 1024 * 1024),
        name="extras",
    )(own, other)


def solution(mesh):
    in_specs = (
        P("rows", None),
        P("rows", None, None, None),
        P("rows", None),
        P("rows"),
        P(),
        P(),
        P("rows", None),
    )
    out_specs = (P("rows", None), P(), P(), P("rows", None))
    return jax.shard_map(
        on_device, mesh=mesh, in_specs=in_specs, out_specs=out_specs, check_vma=False
    )
```

```python
import functools

import jax
import jax.numpy as jnp
import numpy as np
from jax import lax
from jax.experimental import pallas as pl
from jax.experimental.pallas import tpu as pltpu
from jax.sharding import PartitionSpec as P

AXIS = "rows"
SIZES = (4, 4, 4, 2)
Y, X, Z = 0, 1, 2
PLANES = ((Y, Z), (Y, X))
LINE = (X, Z)
STEPS = ((Y, Z), (X, Y))
BF16 = jnp.bfloat16
F32 = jnp.float32
GROUP = 8
STARTS = ((0,), (16, 56), (24, 48), (32,), (40,))
AROUND = (2, 3, 1)
DB = 16


def device(at):
    return int(np.ravel_multi_index([t % n for t, n in zip(at, SIZES)], SIZES))


def groups(axes):
    out = {}
    for i in range(128):
        at = [int(v) for v in np.unravel_index(i, SIZES)]
        own = axes[at[3]]
        key = tuple(-1 if a in own else at[a] for a in range(4))
        out.setdefault(key, []).append((tuple(at[a] for a in own), i))
    return [[i for _, i in sorted(members)] for _, members in sorted(out.items())]


def exchange(x, axes):
    return lax.all_to_all(
        x, AXIS, split_axis=0, concat_axis=0, tiled=True, axis_index_groups=groups(axes)
    )


def pairs(move):
    return [(i, device(move([int(v) for v in np.unravel_index(i, SIZES)]))) for i in range(128)]


def hop(x, axes, k):
    def move(at):
        at[axes[at[3]]] += k
        return at

    return lax.ppermute(x, AXIS, pairs(move))


def around(x, axes):
    return [hop(x, axes, k) for k in AROUND]


def swap(x):
    def move(at):
        at[3] += 1
        return at

    return lax.ppermute(x, AXIS, pairs(move))


def dot(a, b, dims):
    return lax.dot_general(a, b, (dims, ((), ())), preferred_element_type=F32)


def load_kernel(a_hbm, a_ref, sem):
    copies = [
        pltpu.make_async_copy(a_hbm.at[s], a_ref.at[:, pl.ds(s * 512, 512)], sem.at[s])
        for s in range(16)
    ]
    for copy in copies:
        copy.start()
    for copy in copies:
        copy.wait()


def load(values):
    return pl.pallas_call(
        load_kernel,
        out_shape=pltpu.VMEM((512, 8192), BF16),
        in_specs=[pl.BlockSpec(memory_space=pltpu.HBM)],
        out_specs=pl.BlockSpec(memory_space=pltpu.VMEM),
        scratch_shapes=[pltpu.SemaphoreType.DMA((16,))],
        compiler_params=pltpu.CompilerParams(vmem_limit_bytes=1024 * 1024),
        cost_estimate=pl.CostEstimate(flops=0, bytes_accessed=2 * 8 * 2**20, transcendentals=0),
        name="load",
    )(pltpu.with_memory_space_constraint(values, pltpu.HBM))


def kernel(
    col_ref, count_ref, a_ref, w_ref, b_ref, cot_ref, _zeros, *rest,
):
    blocks, (act_ref, r_ref, e_ref, g_buf, x_buf, acc, g_t) = rest[:10], rest[10:]
    count = count_ref[0]
    index = lax.axis_index(AXIS)
    me = (index >> 5, (index >> 3) & 3, (index >> 1) & 3)
    core = index & 1

    def there(t, zlo):
        return lax.shift_right_logical(t, 3), lax.shift_right_logical(t, 1) & 3, (t & 1) * 2 + zlo

    def source(t, zlo, cc):
        at = there(t, zlo)
        away = [(at[i] - me[i]) & 3 for i in range(3)]
        first, second = [
            sum(jnp.where(away[i] == 4 - k, place + 1, 0) for place, k in enumerate(AROUND))
            for i in STEPS[cc]
        ]
        return (-away[LINE[cc]] & 3) * 16 + second * 4 + first

    def target(t, zlo, cc):
        at = there(t, zlo)
        away = [(at[i] - me[i]) & 3 for i in range(3)]
        first, second = STEPS[cc]
        return away[LINE[cc]], away[second] * 4 + away[first]

    for side in range(2):
        for ref, starts in zip(blocks[side * 5 : side * 5 + 5], STARTS):
            length = ref.shape[0] // len(starts)
            for i, start in enumerate(starts):
                g_buf[side, start : start + length] = ref[i * length : i * length + length]
    acc[...] = jnp.zeros_like(acc)

    def forward(g, carry):
        for q in range(GROUP):
            s = g * GROUP + q
            t = col_ref[0, s]
            live = s < count
            for j in range(4):
                cc = j % 2
                at = source(t, j // 2, cc)
                piece = g_buf[jnp.where(core == cc, 0, 1), at]
                rows = slice(q * 512 + j * 128, q * 512 + j * 128 + 128)
                x_buf[rows] = jnp.where(live, piece, jnp.zeros_like(piece))
        columns = pl.ds(pl.multiple_of(g * (GROUP * 512), GROUP * 512), GROUP * 512)
        acc[...] += dot(a_ref[:, columns], x_buf[...], ((1,), (0,)))
        return carry

    lax.fori_loop(0, 16 // GROUP, forward, 0)

    agg = acc[...].astype(BF16)
    pre = dot(agg, w_ref[...], ((1,), (0,))) + b_ref[...]
    low = jnp.exp(jnp.minimum(pre, 0.0))
    act_ref[...] = jnp.where(pre > 0, pre, low - 1.0).astype(BF16)
    grad = (cot_ref[...].astype(F32) * low).astype(BF16)
    g_t[...] = grad.astype(F32).T.astype(BF16)
    dw = dot(agg, grad, ((0,), (0,)))
    db = jnp.sum(grad.astype(F32), axis=0, keepdims=True)
    for h in range(2):
        half = slice(h * 128, h * 128 + 128)
        side = jnp.where(core == h, 0, 1)
        e_ref[side, :256] = dw[:, half]
        e_ref[side, 256:] = jnp.broadcast_to(db[:, half], (8, 128))

    def backward(g, carry):
        for q in range(GROUP):
            s = g * GROUP + q
            t = col_ref[0, s]
            columns = pl.ds(pl.multiple_of(s * 512, 512), 512)
            part = dot(g_t[...], a_ref[:, columns], ((1,), (0,)))
            part = jnp.where(s < count, part, 0.0).astype(BF16)
            for j in range(4):
                cc = j % 2
                k3, k21 = target(t, j // 2, cc)
                rows = pl.ds(pl.multiple_of(k21 * 256, 256), 256)
                other = jnp.where(k3 == 0, 7, jnp.where(k3 == 1, 5, jnp.where(k3 == 2, 4, 6)))
                r_ref[jnp.where(core == cc, k3, other), rows] = part[:, j * 128 : j * 128 + 128]
        return carry

    lax.fori_loop(0, 16 // GROUP, backward, 0)


def clear(_after, zeros):
    zeros[...] = jnp.zeros_like(zeros)


def local(cols, count, values, weight, bias, cotangent, zeros, blocks):
    vmem = pl.BlockSpec(memory_space=pltpu.VMEM)
    return pl.pallas_call(
        kernel,
        out_shape=(
            pltpu.VMEM((512, 256), BF16),
            pltpu.VMEM((8, 4096, 128), BF16),
            pltpu.VMEM((2, 264, 128), F32),
        ),
        in_specs=[pl.BlockSpec(memory_space=pltpu.SMEM)] * 2 + [vmem] * 15,
        out_specs=(vmem,) * 3,
        input_output_aliases={6: 1},
        scratch_shapes=[
            pltpu.VMEM((2, 64, 128, 256), BF16),
            pltpu.VMEM((GROUP * 512, 256), BF16),
            pltpu.VMEM((512, 256), F32),
            pltpu.VMEM((256, 512), BF16),
        ],
        compiler_params=pltpu.CompilerParams(vmem_limit_bytes=18 * 1024 * 1024),
        cost_estimate=pl.CostEstimate(
            flops=2 * 2 * 16 * 512 * 512 * 256, bytes_accessed=8 * 2**20, transcendentals=512 * 256
        ),
        name="layer",
    )(cols, count, values, weight, bias, cotangent, zeros, *blocks)


def in_vmem(name, body, outs, *ins, last=False):
    vmem = pl.BlockSpec(memory_space=pltpu.VMEM)
    size = sum(int(np.prod(o.shape)) * 2 for o in (*outs, *ins))
    return pl.pallas_call(
        body,
        out_shape=tuple(o if last else pltpu.VMEM(o.shape, o.dtype) for o in outs),
        in_specs=[vmem] * len(ins),
        out_specs=(vmem,) * len(outs),
        compiler_params=pltpu.CompilerParams(vmem_limit_bytes=4 * 1024 * 1024),
        cost_estimate=pl.CostEstimate(flops=0, bytes_accessed=size // 4, transcendentals=0),
        name=name,
    )(*ins)


def like(*shape, dtype=BF16):
    return jax.ShapeDtypeStruct(shape, dtype)


def widened(*parts):
    total = parts[0].astype(F32)
    for part in parts[1:]:
        total = total + part.astype(F32)
    return total


def join(*parts):
    def body(*refs):
        at = 0
        for ref in refs[:-1]:
            refs[-1][at : at + ref.shape[0]] = ref[...]
            at += ref.shape[0]

    rows = sum(p.shape[0] for p in parts)
    return in_vmem("join", body, [like(rows, *parts[0].shape[1:])], *parts)[0]


def halves(x, lower, upper):
    lower[...] = x[:8]
    upper[...] = x[8:]


def add_rows(o, start, *parts):
    o[start : start + 256] = widened(*[ref[at : at + 256] for ref, at in parts]).astype(BF16)


def split(v):
    hi = v.astype(BF16).astype(F32)
    return hi, v - hi


def first_terms(r, t, e, te, o1, o3, ride):
    total = e[0] + te[...]
    hi, low = split(total[256:])
    ride[:256] = total[:256].astype(BF16)
    ride[256:] = jnp.concatenate([hi, low]).astype(BF16)
    for at in range(0, 2048, 256):
        add_rows(o1, at, (r.at[2], at), (t, at))
        add_rows(o3, at, (r.at[2], at + 2048), (t, at + 2048))
    o1[2048:] = ride[...]
    o3[2048:] = ride[...]


def extra_pieces(e, te, via1, via3, far, o):
    total = e[0] + te[...]
    dw = total[:256] + widened(via1[2048:2304], via3[2048:2304], far[:256])
    db = total[256:] + widened(via1[2304:2312], via1[2312:], via3[2304:2312], via3[2312:], far[256:264], far[264:])
    for i in range(16):
        o[i, :DB] = dw[i * 16 : i * 16 + 16]
        o[i, DB:] = db


def second_terms(r, t, via1, via3, _pieces, p1, p3):
    for at in range(0, 2048, 256):
        up = at + 2048
        add_rows(p1, at, (r.at[1], at), (t.at[0], at), (via1, at))
        add_rows(p1, up, (r.at[1], up), (t.at[0], up))
        add_rows(p3, at, (r.at[3], at), (t.at[1], at))
        add_rows(p3, up, (r.at[3], up), (t.at[1], up), (via3, at))


def line_sum(r, t0, p1, p3, got, own, piece, m1, m2, m3):
    total = got[0]
    for i in range(1, 16):
        total = total + got[i]
    total = total * 65536 ** (-0.5)
    hi, low = split(total[DB:])
    piece[...] = jnp.concatenate([total[:DB], hi, low]).astype(BF16)
    for k, message in enumerate((None, m1, m2, m3)):
        for at in range(0, 1024, 256):
            rows = slice(k * 1024 + at, k * 1024 + at + 256)
            terms = widened(r[0, rows], t0[rows], p1[rows], p3[rows])
            if message is None:
                own[at : at + 256] = terms
            else:
                message[at : at + 256] = terms.astype(BF16)
        if message is not None:
            message[1024:] = piece[...]


def plane_sum(own, piece, g2, g1, g3, rest, pieces, n1, n2, n3):
    for i, ref in enumerate((piece, g1, g2, g3)):
        pieces[i * 32 : i * 32 + 32] = ref[-32:]
    for k, message in enumerate((None, n1, n2, n3)):
        rows = slice(k * 256, k * 256 + 256)
        terms = own[rows] + widened(g1[rows], g2[rows], g3[rows])
        if message is None:
            rest[...] = terms
        else:
            message[:256] = terms.astype(BF16)
            message[256:] = pieces[...]


def extra_half(pieces, h2, h1, h3, o):
    index = lax.axis_index(AXIS)
    at = (index >> 5, (index >> 3) & 3, (index >> 1) & 3)

    def choose(axes):
        return jnp.where((index & 1) == 0, at[axes[0]], at[axes[1]])

    first, second = (choose(axes) for axes in zip(*STEPS))
    flip = [STEPS[c] != PLANES[c] for c in range(2)]
    flip = jnp.where((index & 1) == 0, int(flip[0]), int(flip[1])) == 1
    for k1, (ref, base) in enumerate(((pieces, 0), (h1, 256), (h2, 256), (h3, 256))):
        for k2 in range(4):
            i, j = (first - k1) & 3, (second - k2) & 3
            place = jnp.where(flip, j * 4 + i, i * 4 + j)
            start = base + k2 * 32
            o[pl.ds(pl.multiple_of(place * 16, 16), 16)] = ref[start : start + DB].astype(F32)
    o[256:] = widened(pieces[DB : DB + 8], pieces[DB + 8 : DB + 16])


def extra_both(core, own, other, dw, db):
    here = core == 0
    first = jnp.where(here, own[...], other[...])
    second = jnp.where(here, other[...], own[...])
    dw[:, :128], dw[:, 128:] = first[:256], second[:256]
    db[:, :128], db[:, 128:] = first[256:257], second[256:257]


def finish(rest, h2, h1, h3, w, o):
    total = rest[...] + widened(h1[:256], h2[:256], h3[:256])
    o[...] = dot(total.T.astype(BF16), w[...], ((1,), (1,)))


def keep(x_ref, o_ref, sem):
    copy = pltpu.make_async_copy(x_ref, o_ref, sem)
    copy.start()
    copy.wait()


def to_output(x):
    return pl.pallas_call(
        keep,
        out_shape=like(*x.shape),
        in_specs=[pl.BlockSpec(memory_space=pltpu.VMEM)],
        out_specs=pl.BlockSpec(memory_space=pltpu.HBM),
        scratch_shapes=[pltpu.SemaphoreType.DMA],
        compiler_params=pltpu.CompilerParams(vmem_limit_bytes=1024 * 1024),
        name="to_output",
    )(x)


def on_device(features, tile_values, tile_col, tile_count, weight, bias, cotangent):
    values = load(tile_values[0])
    held = features[None]
    first, second = zip(*STEPS)
    held = join(held, *around(held, first))
    held, values = lax.optimization_barrier((held, values))
    zeros = in_vmem("clear", clear, [like(8, 4096, 128)], held)[0]
    held = join(held, *around(held, second))
    held, zeros = lax.optimization_barrier((held, zeros))
    h1, h2 = in_vmem("halves", halves, [like(8, 128, 256)] * 2, held)
    a1, b2, a2, b1 = hop(h1, LINE, 1), hop(h2, LINE, 3), hop(h2, LINE, 1), hop(h1, LINE, 3)
    a1, b2, other = lax.optimization_barrier((a1, b2, held))
    c1, c2 = hop(a1, LINE, 1), hop(b2, LINE, 3)
    mine = [held, join(a1, b2), join(a2, b1), c1, c2]
    theirs = [swap(other)] + [swap(g) for g in mine[1:]]
    activation, r_all, e_all = local(
        tile_col, tile_count, values, weight, bias[None], cotangent, zeros, mine + theirs
    )

    some, whole = like(2048 + 272, 128), like(4096, 128)
    e_theirs = swap(e_all[1])
    o1, o3, ride = in_vmem(
        "first_terms", first_terms, [some, some, like(272, 128)],
        r_all, swap(r_all[4]), e_all, e_theirs,
    )
    o1, o3, ride, beside, activation = lax.optimization_barrier(
        (o1, o3, ride, r_all[5:7], activation)
    )
    via1, via3, far = hop(o1, LINE, 1), hop(o3, LINE, 3), hop(ride, LINE, 2)
    beside = swap(beside)
    activation = to_output(activation)
    pieces = in_vmem(
        "extra_pieces", extra_pieces, [like(16, 24, 128, dtype=F32)],
        e_all, e_theirs, via1, via3, far,
    )[0]
    p1, p3 = in_vmem(
        "second_terms", second_terms, [whole, whole], r_all, beside, via1, via3, pieces
    )
    p1, p3, pieces, activation, own = lax.optimization_barrier(
        (p1, p3, pieces, activation, r_all[7])
    )
    p1, p3 = hop(p1, LINE, 1), hop(p3, LINE, 3)
    pieces = exchange(pieces, PLANES)
    own, piece, *sent = in_vmem(
        "line_sum", line_sum, [like(1024, 128, dtype=F32), like(32, 128)] + [like(1056, 128)] * 3,
        r_all, swap(own), p1, p3, pieces,
    )
    got = [hop(sent[k - 1], second, k) for k in (2, 1, 3)]
    rest, pieces, *sent = in_vmem(
        "plane_sum", plane_sum, [like(256, 128, dtype=F32), like(128, 128)] + [like(384, 128)] * 3,
        own, piece, *got,
    )
    got = [hop(sent[k - 1], first, k) for k in (2, 1, 3)]
    own = in_vmem("extra_half", extra_half, [like(264, 128, dtype=F32)], pieces, *got)[0]
    other = swap(own)
    grad_features = in_vmem(
        "finish", finish, [like(128, 256, dtype=F32)], rest, *got, weight, last=True
    )[0]
    grad_weight, grad_bias = extras(own, other)
    return activation, grad_weight, grad_bias[0], grad_features


def extras(own, other):
    vmem = pl.BlockSpec(memory_space=pltpu.VMEM)

    def body(own, other, dw, db):
        extra_both(lax.axis_index(AXIS) & 1, own, other, dw, db)

    return pl.pallas_call(
        body,
        out_shape=(like(256, 256, dtype=F32), like(1, 256, dtype=F32)),
        in_specs=[vmem] * 2,
        out_specs=(vmem,) * 2,
        compiler_params=pltpu.CompilerParams(vmem_limit_bytes=4 * 1024 * 1024),
        name="extras",
    )(own, other)


def solution(mesh):
    in_specs = (
        P("rows", None),
        P("rows", None, None, None),
        P("rows", None),
        P("rows"),
        P(),
        P(),
        P("rows", None),
    )
    out_specs = (P("rows", None), P(), P(), P("rows", None))
    return jax.shard_map(
        on_device, mesh=mesh, in_specs=in_specs, out_specs=out_specs, check_vma=False
    )
```

```python
import functools

import jax
import jax.numpy as jnp
import numpy as np
from jax import lax
from jax.experimental import pallas as pl
from jax.experimental.pallas import tpu as pltpu
from jax.sharding import PartitionSpec as P

AXIS = "rows"
SIZES = (4, 4, 4, 2)
Y, X, Z = 0, 1, 2
PLANES = ((Y, Z), (Y, X))
LINE = (X, Z)
STEPS = ((Y, Z), (X, Y))
BF16 = jnp.bfloat16
F32 = jnp.float32
GROUP = 8
STARTS = ((0,), (16, 56), (24, 48), (32,), (40,))
AROUND = (2, 3, 1)
DB = 16


def device(at):
    return int(np.ravel_multi_index([t % n for t, n in zip(at, SIZES)], SIZES))


def groups(axes):
    out = {}
    for i in range(128):
        at = [int(v) for v in np.unravel_index(i, SIZES)]
        own = axes[at[3]]
        key = tuple(-1 if a in own else at[a] for a in range(4))
        out.setdefault(key, []).append((tuple(at[a] for a in own), i))
    return [[i for _, i in sorted(members)] for _, members in sorted(out.items())]


def exchange(x, axes):
    return lax.all_to_all(
        x, AXIS, split_axis=0, concat_axis=0, tiled=True, axis_index_groups=groups(axes)
    )


def pairs(move):
    return [(i, device(move([int(v) for v in np.unravel_index(i, SIZES)]))) for i in range(128)]


def hop(x, axes, k):
    def move(at):
        at[axes[at[3]]] += k
        return at

    return lax.ppermute(x, AXIS, pairs(move))


def around(x, axes):
    return [hop(x, axes, k) for k in AROUND]


def swap(x):
    def move(at):
        at[3] += 1
        return at

    return lax.ppermute(x, AXIS, pairs(move))


def dot(a, b, dims):
    return lax.dot_general(a, b, (dims, ((), ())), preferred_element_type=F32)


def load_kernel(a_hbm, a_ref, sem):
    copies = [
        pltpu.make_async_copy(a_hbm.at[s], a_ref.at[:, pl.ds(s * 512, 512)], sem.at[s])
        for s in range(16)
    ]
    for copy in copies:
        copy.start()
    for copy in copies:
        copy.wait()


def load(values):
    return pl.pallas_call(
        load_kernel,
        out_shape=pltpu.VMEM((512, 8192), BF16),
        in_specs=[pl.BlockSpec(memory_space=pltpu.HBM)],
        out_specs=pl.BlockSpec(memory_space=pltpu.VMEM),
        scratch_shapes=[pltpu.SemaphoreType.DMA((16,))],
        compiler_params=pltpu.CompilerParams(vmem_limit_bytes=1024 * 1024),
        cost_estimate=pl.CostEstimate(flops=0, bytes_accessed=2 * 8 * 2**20, transcendentals=0),
        name="load",
    )(pltpu.with_memory_space_constraint(values, pltpu.HBM))


def kernel(
    col_ref, count_ref, a_ref, w_ref, b_ref, cot_ref, _zeros, *rest,
):
    blocks, (act_ref, r_ref, e_ref, g_buf, x_buf, acc, g_t) = rest[:10], rest[10:]
    count = count_ref[0]
    index = lax.axis_index(AXIS)
    me = (index >> 5, (index >> 3) & 3, (index >> 1) & 3)
    core = index & 1

    def there(t, zlo):
        return lax.shift_right_logical(t, 3), lax.shift_right_logical(t, 1) & 3, (t & 1) * 2 + zlo

    def source(t, zlo, cc):
        at = there(t, zlo)
        away = [(at[i] - me[i]) & 3 for i in range(3)]
        first, second = [
            sum(jnp.where(away[i] == 4 - k, place + 1, 0) for place, k in enumerate(AROUND))
            for i in STEPS[cc]
        ]
        return (-away[LINE[cc]] & 3) * 16 + second * 4 + first

    def target(t, zlo, cc):
        at = there(t, zlo)
        away = [(at[i] - me[i]) & 3 for i in range(3)]
        first, second = STEPS[cc]
        return away[LINE[cc]], away[second] * 4 + away[first]

    for side in range(2):
        for ref, starts in zip(blocks[side * 5 : side * 5 + 5], STARTS):
            length = ref.shape[0] // len(starts)
            for i, start in enumerate(starts):
                g_buf[side, start : start + length] = ref[i * length : i * length + length]
    def forward(g):
        for q in range(GROUP):
            s = g * GROUP + q
            t = col_ref[0, s]
            live = s < count
            for j in range(4):
                cc = j % 2
                at = source(t, j // 2, cc)
                piece = g_buf[jnp.where(core == cc, 0, 1), at]
                rows = slice(q * 512 + j * 128, q * 512 + j * 128 + 128)
                x_buf[rows] = jnp.where(live, piece, jnp.zeros_like(piece))
        columns = slice(g * GROUP * 512, (g + 1) * GROUP * 512)
        return dot(a_ref[:, columns], x_buf[...], ((1,), (0,)))

    acc[...] = forward(0)
    acc[...] += forward(1)

    agg = acc[...].astype(BF16)
    pre = dot(agg, w_ref[...], ((1,), (0,))) + b_ref[...]
    low = jnp.exp(jnp.minimum(pre, 0.0))
    act_ref[...] = jnp.where(pre > 0, pre, low - 1.0).astype(BF16)
    grad = (cot_ref[...].astype(F32) * low).astype(BF16)
    g_t[...] = grad.astype(F32).T.astype(BF16)
    dw = dot(agg, grad, ((0,), (0,)))
    db = jnp.sum(grad.astype(F32), axis=0, keepdims=True)
    for h in range(2):
        half = slice(h * 128, h * 128 + 128)
        side = jnp.where(core == h, 0, 1)
        e_ref[side, :256] = dw[:, half]
        e_ref[side, 256:] = jnp.broadcast_to(db[:, half], (8, 128))

    def backward(g, carry):
        for q in range(GROUP):
            s = g * GROUP + q
            t = col_ref[0, s]
            columns = pl.ds(pl.multiple_of(s * 512, 512), 512)
            part = dot(g_t[...], a_ref[:, columns], ((1,), (0,)))
            part = jnp.where(s < count, part, 0.0).astype(BF16)
            for j in range(4):
                cc = j % 2
                k3, k21 = target(t, j // 2, cc)
                rows = pl.ds(pl.multiple_of(k21 * 256, 256), 256)
                other = jnp.where(k3 == 0, 7, jnp.where(k3 == 1, 5, jnp.where(k3 == 2, 4, 6)))
                r_ref[jnp.where(core == cc, k3, other), rows] = part[:, j * 128 : j * 128 + 128]
        return carry

    lax.fori_loop(0, 16 // GROUP, backward, 0)


def clear(_after, zeros):
    zeros[...] = jnp.zeros_like(zeros)


def local(cols, count, values, weight, bias, cotangent, zeros, blocks):
    vmem = pl.BlockSpec(memory_space=pltpu.VMEM)
    return pl.pallas_call(
        kernel,
        out_shape=(
            pltpu.VMEM((512, 256), BF16),
            pltpu.VMEM((8, 4096, 128), BF16),
            pltpu.VMEM((2, 264, 128), F32),
        ),
        in_specs=[pl.BlockSpec(memory_space=pltpu.SMEM)] * 2 + [vmem] * 15,
        out_specs=(vmem,) * 3,
        input_output_aliases={6: 1},
        scratch_shapes=[
            pltpu.VMEM((2, 64, 128, 256), BF16),
            pltpu.VMEM((GROUP * 512, 256), BF16),
            pltpu.VMEM((512, 256), F32),
            pltpu.VMEM((256, 512), BF16),
        ],
        compiler_params=pltpu.CompilerParams(vmem_limit_bytes=18 * 1024 * 1024),
        cost_estimate=pl.CostEstimate(
            flops=2 * 2 * 16 * 512 * 512 * 256, bytes_accessed=8 * 2**20, transcendentals=512 * 256
        ),
        name="layer",
    )(cols, count, values, weight, bias, cotangent, zeros, *blocks)


def in_vmem(name, body, outs, *ins, last=False):
    vmem = pl.BlockSpec(memory_space=pltpu.VMEM)
    size = sum(int(np.prod(o.shape)) * 2 for o in (*outs, *ins))
    return pl.pallas_call(
        body,
        out_shape=tuple(o if last else pltpu.VMEM(o.shape, o.dtype) for o in outs),
        in_specs=[vmem] * len(ins),
        out_specs=(vmem,) * len(outs),
        compiler_params=pltpu.CompilerParams(vmem_limit_bytes=4 * 1024 * 1024),
        cost_estimate=pl.CostEstimate(flops=0, bytes_accessed=size // 4, transcendentals=0),
        name=name,
    )(*ins)


def like(*shape, dtype=BF16):
    return jax.ShapeDtypeStruct(shape, dtype)


def widened(*parts):
    total = parts[0].astype(F32)
    for part in parts[1:]:
        total = total + part.astype(F32)
    return total


def join(*parts):
    def body(*refs):
        at = 0
        for ref in refs[:-1]:
            refs[-1][at : at + ref.shape[0]] = ref[...]
            at += ref.shape[0]

    rows = sum(p.shape[0] for p in parts)
    return in_vmem("join", body, [like(rows, *parts[0].shape[1:])], *parts)[0]


def halves(x, lower, upper):
    lower[...] = x[:8]
    upper[...] = x[8:]


def add_rows(o, start, *parts):
    o[start : start + 256] = widened(*[ref[at : at + 256] for ref, at in parts]).astype(BF16)


def split(v):
    hi = v.astype(BF16).astype(F32)
    return hi, v - hi


def first_terms(r, t, e, te, o1, o3, ride):
    total = e[0] + te[...]
    hi, low = split(total[256:])
    ride[:256] = total[:256].astype(BF16)
    ride[256:] = jnp.concatenate([hi, low]).astype(BF16)
    for at in range(0, 2048, 256):
        add_rows(o1, at, (r.at[2], at), (t, at))
        add_rows(o3, at, (r.at[2], at + 2048), (t, at + 2048))
    o1[2048:] = ride[...]
    o3[2048:] = ride[...]


def extra_pieces(e, te, via1, via3, far, o):
    total = e[0] + te[...]
    dw = total[:256] + widened(via1[2048:2304], via3[2048:2304], far[:256])
    db = total[256:] + widened(via1[2304:2312], via1[2312:], via3[2304:2312], via3[2312:], far[256:264], far[264:])
    for i in range(16):
        o[i, :DB] = dw[i * 16 : i * 16 + 16]
        o[i, DB:] = db


def second_terms(r, t, via1, via3, _pieces, p1, p3):
    for at in range(0, 2048, 256):
        up = at + 2048
        add_rows(p1, at, (r.at[1], at), (t.at[0], at), (via1, at))
        add_rows(p1, up, (r.at[1], up), (t.at[0], up))
        add_rows(p3, at, (r.at[3], at), (t.at[1], at))
        add_rows(p3, up, (r.at[3], up), (t.at[1], up), (via3, at))


def line_sum(r, t0, p1, p3, got, own, piece, m1, m2, m3):
    total = got[0]
    for i in range(1, 16):
        total = total + got[i]
    total = total * 65536 ** (-0.5)
    hi, low = split(total[DB:])
    piece[...] = jnp.concatenate([total[:DB], hi, low]).astype(BF16)
    for k, message in enumerate((None, m1, m2, m3)):
        for at in range(0, 1024, 256):
            rows = slice(k * 1024 + at, k * 1024 + at + 256)
            terms = widened(r[0, rows], t0[rows], p1[rows], p3[rows])
            if message is None:
                own[at : at + 256] = terms
            else:
                message[at : at + 256] = terms.astype(BF16)
        if message is not None:
            message[1024:] = piece[...]


def plane_sum(own, piece, g2, g1, g3, rest, pieces, n1, n2, n3):
    for i, ref in enumerate((piece, g1, g2, g3)):
        pieces[i * 32 : i * 32 + 32] = ref[-32:]
    for k, message in enumerate((None, n1, n2, n3)):
        rows = slice(k * 256, k * 256 + 256)
        terms = own[rows] + widened(g1[rows], g2[rows], g3[rows])
        if message is None:
            rest[...] = terms
        else:
            message[:256] = terms.astype(BF16)
            message[256:] = pieces[...]


def extra_half(pieces, h2, h1, h3, o):
    index = lax.axis_index(AXIS)
    at = (index >> 5, (index >> 3) & 3, (index >> 1) & 3)

    def choose(axes):
        return jnp.where((index & 1) == 0, at[axes[0]], at[axes[1]])

    first, second = (choose(axes) for axes in zip(*STEPS))
    flip = [STEPS[c] != PLANES[c] for c in range(2)]
    flip = jnp.where((index & 1) == 0, int(flip[0]), int(flip[1])) == 1
    for k1, (ref, base) in enumerate(((pieces, 0), (h1, 256), (h2, 256), (h3, 256))):
        for k2 in range(4):
            i, j = (first - k1) & 3, (second - k2) & 3
            place = jnp.where(flip, j * 4 + i, i * 4 + j)
            start = base + k2 * 32
            o[pl.ds(pl.multiple_of(place * 16, 16), 16)] = ref[start : start + DB].astype(F32)
    o[256:] = widened(pieces[DB : DB + 8], pieces[DB + 8 : DB + 16])


def extra_both(core, own, other, dw, db):
    here = core == 0
    first = jnp.where(here, own[...], other[...])
    second = jnp.where(here, other[...], own[...])
    dw[:, :128], dw[:, 128:] = first[:256], second[:256]
    db[:, :128], db[:, 128:] = first[256:257], second[256:257]


def finish(rest, h2, h1, h3, w, o):
    total = rest[...] + widened(h1[:256], h2[:256], h3[:256])
    o[...] = dot(total.T.astype(BF16), w[...], ((1,), (1,)))


def keep(x_ref, o_ref, sem):
    copy = pltpu.make_async_copy(x_ref, o_ref, sem)
    copy.start()
    copy.wait()


def to_output(x):
    return pl.pallas_call(
        keep,
        out_shape=like(*x.shape),
        in_specs=[pl.BlockSpec(memory_space=pltpu.VMEM)],
        out_specs=pl.BlockSpec(memory_space=pltpu.HBM),
        scratch_shapes=[pltpu.SemaphoreType.DMA],
        compiler_params=pltpu.CompilerParams(vmem_limit_bytes=1024 * 1024),
        name="to_output",
    )(x)


def on_device(features, tile_values, tile_col, tile_count, weight, bias, cotangent):
    values = load(tile_values[0])
    held = features[None]
    first, second = zip(*STEPS)
    held = join(held, *around(held, first))
    held, values = lax.optimization_barrier((held, values))
    zeros = in_vmem("clear", clear, [like(8, 4096, 128)], held)[0]
    held = join(held, *around(held, second))
    held, zeros = lax.optimization_barrier((held, zeros))
    h1, h2 = in_vmem("halves", halves, [like(8, 128, 256)] * 2, held)
    a1, b2, a2, b1 = hop(h1, LINE, 1), hop(h2, LINE, 3), hop(h2, LINE, 1), hop(h1, LINE, 3)
    a1, b2, other = lax.optimization_barrier((a1, b2, held))
    c1, c2 = hop(a1, LINE, 1), hop(b2, LINE, 3)
    mine = [held, join(a1, b2), join(a2, b1), c1, c2]
    theirs = [swap(other)] + [swap(g) for g in mine[1:]]
    activation, r_all, e_all = local(
        tile_col, tile_count, values, weight, bias[None], cotangent, zeros, mine + theirs
    )

    some, whole = like(2048 + 272, 128), like(4096, 128)
    e_theirs = swap(e_all[1])
    o1, o3, ride = in_vmem(
        "first_terms", first_terms, [some, some, like(272, 128)],
        r_all, swap(r_all[4]), e_all, e_theirs,
    )
    o1, o3, ride, beside, activation = lax.optimization_barrier(
        (o1, o3, ride, r_all[5:7], activation)
    )
    via1, via3, far = hop(o1, LINE, 1), hop(o3, LINE, 3), hop(ride, LINE, 2)
    beside = swap(beside)
    activation = to_output(activation)
    pieces = in_vmem(
        "extra_pieces", extra_pieces, [like(16, 24, 128, dtype=F32)],
        e_all, e_theirs, via1, via3, far,
    )[0]
    p1, p3 = in_vmem(
        "second_terms", second_terms, [whole, whole], r_all, beside, via1, via3, pieces
    )
    p1, p3, pieces, activation, own = lax.optimization_barrier(
        (p1, p3, pieces, activation, r_all[7])
    )
    p1, p3 = hop(p1, LINE, 1), hop(p3, LINE, 3)
    pieces = exchange(pieces, PLANES)
    own, piece, *sent = in_vmem(
        "line_sum", line_sum, [like(1024, 128, dtype=F32), like(32, 128)] + [like(1056, 128)] * 3,
        r_all, swap(own), p1, p3, pieces,
    )
    got = [hop(sent[k - 1], second, k) for k in (2, 1, 3)]
    rest, pieces, *sent = in_vmem(
        "plane_sum", plane_sum, [like(256, 128, dtype=F32), like(128, 128)] + [like(384, 128)] * 3,
        own, piece, *got,
    )
    got = [hop(sent[k - 1], first, k) for k in (2, 1, 3)]
    own = in_vmem("extra_half", extra_half, [like(264, 128, dtype=F32)], pieces, *got)[0]
    other = swap(own)
    grad_features = in_vmem(
        "finish", finish, [like(128, 256, dtype=F32)], rest, *got, weight, last=True
    )[0]
    grad_weight, grad_bias = extras(own, other)
    return activation, grad_weight, grad_bias[0], grad_features


def extras(own, other):
    vmem = pl.BlockSpec(memory_space=pltpu.VMEM)

    def body(own, other, dw, db):
        extra_both(lax.axis_index(AXIS) & 1, own, other, dw, db)

    return pl.pallas_call(
        body,
        out_shape=(like(256, 256, dtype=F32), like(1, 256, dtype=F32)),
        in_specs=[vmem] * 2,
        out_specs=(vmem,) * 2,
        compiler_params=pltpu.CompilerParams(vmem_limit_bytes=4 * 1024 * 1024),
        name="extras",
    )(own, other)


def solution(mesh):
    in_specs = (
        P("rows", None),
        P("rows", None, None, None),
        P("rows", None),
        P("rows"),
        P(),
        P(),
        P("rows", None),
    )
    out_specs = (P("rows", None), P(), P(), P("rows", None))
    return jax.shard_map(
        on_device, mesh=mesh, in_specs=in_specs, out_specs=out_specs, check_vma=False
    )
```

```python
import functools

import jax
import jax.numpy as jnp
import numpy as np
from jax import lax
from jax.experimental import pallas as pl
from jax.experimental.pallas import tpu as pltpu
from jax.sharding import PartitionSpec as P

AXIS = "rows"
SIZES = (4, 4, 4, 2)
Y, X, Z = 0, 1, 2
PLANES = ((Y, Z), (Y, X))
LINE = (X, Z)
STEPS = ((Y, Z), (X, Y))
BF16 = jnp.bfloat16
F32 = jnp.float32
GROUP = 8
STARTS = ((0,), (16, 56), (24, 48), (32,), (40,))
AROUND = (2, 3, 1)
DB = 16


def device(at):
    return int(np.ravel_multi_index([t % n for t, n in zip(at, SIZES)], SIZES))


def groups(axes):
    out = {}
    for i in range(128):
        at = [int(v) for v in np.unravel_index(i, SIZES)]
        own = axes[at[3]]
        key = tuple(-1 if a in own else at[a] for a in range(4))
        out.setdefault(key, []).append((tuple(at[a] for a in own), i))
    return [[i for _, i in sorted(members)] for _, members in sorted(out.items())]


def exchange(x, axes):
    return lax.all_to_all(
        x, AXIS, split_axis=0, concat_axis=0, tiled=True, axis_index_groups=groups(axes)
    )


def pairs(move):
    return [(i, device(move([int(v) for v in np.unravel_index(i, SIZES)]))) for i in range(128)]


def hop(x, axes, k):
    def move(at):
        at[axes[at[3]]] += k
        return at

    return lax.ppermute(x, AXIS, pairs(move))


def around(x, axes):
    return [hop(x, axes, k) for k in AROUND]


def swap(x):
    def move(at):
        at[3] += 1
        return at

    return lax.ppermute(x, AXIS, pairs(move))


def dot(a, b, dims):
    return lax.dot_general(a, b, (dims, ((), ())), preferred_element_type=F32)


def load_kernel(a_hbm, a_ref, sem):
    copies = [
        pltpu.make_async_copy(a_hbm.at[s], a_ref.at[:, pl.ds(s * 512, 512)], sem.at[s])
        for s in range(16)
    ]
    for copy in copies:
        copy.start()
    for copy in copies:
        copy.wait()


def load(values):
    return pl.pallas_call(
        load_kernel,
        out_shape=pltpu.VMEM((512, 8192), BF16),
        in_specs=[pl.BlockSpec(memory_space=pltpu.HBM)],
        out_specs=pl.BlockSpec(memory_space=pltpu.VMEM),
        scratch_shapes=[pltpu.SemaphoreType.DMA((16,))],
        compiler_params=pltpu.CompilerParams(vmem_limit_bytes=1024 * 1024),
        cost_estimate=pl.CostEstimate(flops=0, bytes_accessed=2 * 8 * 2**20, transcendentals=0),
        name="load",
    )(pltpu.with_memory_space_constraint(values, pltpu.HBM))


def kernel(
    col_ref, count_ref, a_ref, w_ref, b_ref, cot_ref, _zeros, *rest,
):
    blocks, (act_ref, r_ref, e_ref, g_buf, x_buf, acc, g_t) = rest[:10], rest[10:]
    count = count_ref[0]
    index = lax.axis_index(AXIS)
    me = (index >> 5, (index >> 3) & 3, (index >> 1) & 3)
    core = index & 1

    def there(t, zlo):
        return lax.shift_right_logical(t, 3), lax.shift_right_logical(t, 1) & 3, (t & 1) * 2 + zlo

    def source(t, zlo, cc):
        at = there(t, zlo)
        away = [(at[i] - me[i]) & 3 for i in range(3)]
        first, second = [
            sum(jnp.where(away[i] == 4 - k, place + 1, 0) for place, k in enumerate(AROUND))
            for i in STEPS[cc]
        ]
        return (-away[LINE[cc]] & 3) * 16 + second * 4 + first

    def target(t, zlo, cc):
        at = there(t, zlo)
        away = [(at[i] - me[i]) & 3 for i in range(3)]
        first, second = STEPS[cc]
        return away[LINE[cc]], away[second] * 4 + away[first]

    for side in range(2):
        for ref, starts in zip(blocks[side * 5 : side * 5 + 5], STARTS):
            length = ref.shape[0] // len(starts)
            for i, start in enumerate(starts):
                g_buf[side, start : start + length] = ref[i * length : i * length + length]
    def forward(g):
        for q in range(GROUP):
            s = g * GROUP + q
            t = col_ref[0, s]
            live = s < count
            for j in range(4):
                cc = j % 2
                at = source(t, j // 2, cc)
                piece = g_buf[jnp.where(core == cc, 0, 1), at]
                rows = slice(q * 512 + j * 128, q * 512 + j * 128 + 128)
                x_buf[rows] = jnp.where(live, piece, jnp.zeros_like(piece))
        columns = slice(g * GROUP * 512, (g + 1) * GROUP * 512)
        return dot(a_ref[:, columns], x_buf[...], ((1,), (0,)))

    acc[...] = forward(0)
    acc[...] += forward(1)

    agg = acc[...].astype(BF16)
    pre = dot(agg, w_ref[...], ((1,), (0,))) + b_ref[...]
    low = jnp.exp(jnp.minimum(pre, 0.0))
    act_ref[...] = jnp.where(pre > 0, pre, low - 1.0).astype(BF16)
    grad = (cot_ref[...].astype(F32) * low).astype(BF16)
    g_t[...] = grad.astype(F32).T.astype(BF16)
    dw = dot(agg, grad, ((0,), (0,)))
    db = jnp.sum(grad.astype(F32), axis=0, keepdims=True)
    for h in range(2):
        half = slice(h * 128, h * 128 + 128)
        side = jnp.where(core == h, 0, 1)
        e_ref[side, :256] = dw[:, half]
        e_ref[side, 256:] = jnp.broadcast_to(db[:, half], (8, 128))

    def backward(g, carry):
        for q in range(GROUP):
            s = g * GROUP + q
            t = col_ref[0, s]
            columns = pl.ds(pl.multiple_of(s * 512, 512), 512)
            part = dot(g_t[...], a_ref[:, columns], ((1,), (0,)))
            part = jnp.where(s < count, part, 0.0).astype(BF16)
            for j in range(4):
                cc = j % 2
                k3, k21 = target(t, j // 2, cc)
                rows = pl.ds(pl.multiple_of(k21 * 256, 256), 256)
                other = jnp.where(k3 == 0, 7, jnp.where(k3 == 1, 5, jnp.where(k3 == 2, 4, 6)))
                r_ref[jnp.where(core == cc, k3, other), rows] = part[:, j * 128 : j * 128 + 128]
        return carry

    lax.fori_loop(0, 16 // GROUP, backward, 0)


def clear(_after, zeros):
    zeros[...] = jnp.zeros_like(zeros)


def local(cols, count, values, weight, bias, cotangent, zeros, blocks):
    vmem = pl.BlockSpec(memory_space=pltpu.VMEM)
    return pl.pallas_call(
        kernel,
        out_shape=(
            pltpu.VMEM((512, 256), BF16),
            pltpu.VMEM((8, 4096, 128), BF16),
            pltpu.VMEM((2, 264, 128), F32),
        ),
        in_specs=[pl.BlockSpec(memory_space=pltpu.SMEM)] * 2 + [vmem] * 15,
        out_specs=(vmem,) * 3,
        input_output_aliases={6: 1},
        scratch_shapes=[
            pltpu.VMEM((2, 64, 128, 256), BF16),
            pltpu.VMEM((GROUP * 512, 256), BF16),
            pltpu.VMEM((512, 256), F32),
            pltpu.VMEM((256, 512), BF16),
        ],
        compiler_params=pltpu.CompilerParams(vmem_limit_bytes=18 * 1024 * 1024),
        cost_estimate=pl.CostEstimate(
            flops=2 * 2 * 16 * 512 * 512 * 256, bytes_accessed=8 * 2**20, transcendentals=512 * 256
        ),
        name="layer",
    )(cols, count, values, weight, bias, cotangent, zeros, *blocks)


def in_vmem(name, body, outs, *ins, last=False):
    vmem = pl.BlockSpec(memory_space=pltpu.VMEM)
    size = sum(int(np.prod(o.shape)) * 2 for o in (*outs, *ins))
    return pl.pallas_call(
        body,
        out_shape=tuple(o if last else pltpu.VMEM(o.shape, o.dtype) for o in outs),
        in_specs=[vmem] * len(ins),
        out_specs=(vmem,) * len(outs),
        compiler_params=pltpu.CompilerParams(vmem_limit_bytes=4 * 1024 * 1024),
        cost_estimate=pl.CostEstimate(flops=0, bytes_accessed=size // 4, transcendentals=0),
        name=name,
    )(*ins)


def like(*shape, dtype=BF16):
    return jax.ShapeDtypeStruct(shape, dtype)


def widened(*parts):
    total = parts[0].astype(F32)
    for part in parts[1:]:
        total = total + part.astype(F32)
    return total


def join(*parts):
    def body(*refs):
        at = 0
        for ref in refs[:-1]:
            refs[-1][at : at + ref.shape[0]] = ref[...]
            at += ref.shape[0]

    rows = sum(p.shape[0] for p in parts)
    return in_vmem("join", body, [like(rows, *parts[0].shape[1:])], *parts)[0]


def halves(x, lower, upper):
    lower[...] = x[:8]
    upper[...] = x[8:]


def add_rows(o, start, *parts):
    o[start : start + 256] = widened(*[ref[at : at + 256] for ref, at in parts]).astype(BF16)


def split(v):
    hi = v.astype(BF16).astype(F32)
    return hi, v - hi


def first_terms(r, t, e, te, o1, o3, ride):
    total = e[0] + te[...]
    hi, low = split(total[256:])
    ride[:256] = total[:256].astype(BF16)
    ride[256:] = jnp.concatenate([hi, low]).astype(BF16)
    for at in range(0, 2048, 256):
        add_rows(o1, at, (r.at[2], at), (t, at))
        add_rows(o3, at, (r.at[2], at + 2048), (t, at + 2048))
    o1[2048:] = ride[...]
    o3[2048:] = ride[...]


def extra_pieces(e, te, via1, via3, far, o):
    total = e[0] + te[...]
    dw = total[:256] + widened(via1[2048:2304], via3[2048:2304], far[:256])
    tail = widened(via1[2304:], via3[2304:], far[256:])
    db = total[256:] + tail[:8] + tail[8:]
    for i in range(16):
        o[i, :DB] = dw[i * 16 : i * 16 + 16]
        o[i, DB:] = db


def second_terms(r, t, via1, via3, _pieces, p1, p3):
    for at in range(0, 2048, 256):
        up = at + 2048
        add_rows(p1, at, (r.at[1], at), (t.at[0], at), (via1, at))
        add_rows(p1, up, (r.at[1], up), (t.at[0], up))
        add_rows(p3, at, (r.at[3], at), (t.at[1], at))
        add_rows(p3, up, (r.at[3], up), (t.at[1], up), (via3, at))


def line_sum(r, t0, p1, p3, got, own, piece, m1, m2, m3):
    total = got[0]
    for i in range(1, 16):
        total = total + got[i]
    total = total * 65536 ** (-0.5)
    hi, low = split(total[DB:])
    piece[...] = jnp.concatenate([total[:DB], hi, low]).astype(BF16)
    for k, message in enumerate((None, m1, m2, m3)):
        for at in range(0, 1024, 256):
            rows = slice(k * 1024 + at, k * 1024 + at + 256)
            terms = widened(r[0, rows], t0[rows], p1[rows], p3[rows])
            if message is None:
                own[at : at + 256] = terms
            else:
                message[at : at + 256] = terms.astype(BF16)
        if message is not None:
            message[1024:] = piece[...]


def plane_sum(own, piece, g2, g1, g3, rest, pieces, n1, n2, n3):
    for i, ref in enumerate((piece, g1, g2, g3)):
        pieces[i * 32 : i * 32 + 32] = ref[-32:]
    for k, message in enumerate((None, n1, n2, n3)):
        rows = slice(k * 256, k * 256 + 256)
        terms = own[rows] + widened(g1[rows], g2[rows], g3[rows])
        if message is None:
            rest[...] = terms
        else:
            message[:256] = terms.astype(BF16)
            message[256:] = pieces[...]


def extra_half(pieces, h2, h1, h3, o):
    index = lax.axis_index(AXIS)
    at = (index >> 5, (index >> 3) & 3, (index >> 1) & 3)

    def choose(axes):
        return jnp.where((index & 1) == 0, at[axes[0]], at[axes[1]])

    first, second = (choose(axes) for axes in zip(*STEPS))
    flip = [STEPS[c] != PLANES[c] for c in range(2)]
    flip = jnp.where((index & 1) == 0, int(flip[0]), int(flip[1])) == 1
    for k1, (ref, base) in enumerate(((pieces, 0), (h1, 256), (h2, 256), (h3, 256))):
        for k2 in range(4):
            i, j = (first - k1) & 3, (second - k2) & 3
            place = jnp.where(flip, j * 4 + i, i * 4 + j)
            start = base + k2 * 32
            o[pl.ds(pl.multiple_of(place * 16, 16), 16)] = ref[start : start + DB].astype(F32)
    tail = pieces[DB : DB + 16].astype(F32)
    o[256:] = tail[:8] + tail[8:]


def extra_both(core, own, other, dw, db):
    here = core == 0
    first = jnp.where(here, own[...], other[...])
    second = jnp.where(here, other[...], own[...])
    dw[:, :128], dw[:, 128:] = first[:256], second[:256]
    db[:, :128], db[:, 128:] = first[256:257], second[256:257]


def finish(rest, h2, h1, h3, w, o):
    total = rest[...] + widened(h1[:256], h2[:256], h3[:256])
    o[...] = dot(total.T.astype(BF16), w[...], ((1,), (1,)))


def keep(x_ref, o_ref, sem):
    copy = pltpu.make_async_copy(x_ref, o_ref, sem)
    copy.start()
    copy.wait()


def to_output(x):
    return pl.pallas_call(
        keep,
        out_shape=like(*x.shape),
        in_specs=[pl.BlockSpec(memory_space=pltpu.VMEM)],
        out_specs=pl.BlockSpec(memory_space=pltpu.HBM),
        scratch_shapes=[pltpu.SemaphoreType.DMA],
        compiler_params=pltpu.CompilerParams(vmem_limit_bytes=1024 * 1024),
        name="to_output",
    )(x)


def on_device(features, tile_values, tile_col, tile_count, weight, bias, cotangent):
    values = load(tile_values[0])
    held = features[None]
    first, second = zip(*STEPS)
    held = join(held, *around(held, first))
    held, values = lax.optimization_barrier((held, values))
    zeros = in_vmem("clear", clear, [like(8, 4096, 128)], held)[0]
    held = join(held, *around(held, second))
    held, zeros = lax.optimization_barrier((held, zeros))
    h1, h2 = in_vmem("halves", halves, [like(8, 128, 256)] * 2, held)
    a1, b2, a2, b1 = hop(h1, LINE, 1), hop(h2, LINE, 3), hop(h2, LINE, 1), hop(h1, LINE, 3)
    a1, b2, other = lax.optimization_barrier((a1, b2, held))
    c1, c2 = hop(a1, LINE, 1), hop(b2, LINE, 3)
    mine = [held, join(a1, b2), join(a2, b1), c1, c2]
    theirs = [swap(other)] + [swap(g) for g in mine[1:]]
    activation, r_all, e_all = local(
        tile_col, tile_count, values, weight, bias[None], cotangent, zeros, mine + theirs
    )

    some, whole = like(2048 + 272, 128), like(4096, 128)
    e_theirs = swap(e_all[1])
    o1, o3, ride = in_vmem(
        "first_terms", first_terms, [some, some, like(272, 128)],
        r_all, swap(r_all[4]), e_all, e_theirs,
    )
    o1, o3, ride, beside, activation = lax.optimization_barrier(
        (o1, o3, ride, r_all[5:7], activation)
    )
    via1, via3, far = hop(o1, LINE, 1), hop(o3, LINE, 3), hop(ride, LINE, 2)
    beside = swap(beside)
    activation = to_output(activation)
    pieces = in_vmem(
        "extra_pieces", extra_pieces, [like(16, 24, 128, dtype=F32)],
        e_all, e_theirs, via1, via3, far,
    )[0]
    p1, p3 = in_vmem(
        "second_terms", second_terms, [whole, whole], r_all, beside, via1, via3, pieces
    )
    p1, p3, pieces, activation, own = lax.optimization_barrier(
        (p1, p3, pieces, activation, r_all[7])
    )
    p1, p3 = hop(p1, LINE, 1), hop(p3, LINE, 3)
    pieces = exchange(pieces, PLANES)
    own, piece, *sent = in_vmem(
        "line_sum", line_sum, [like(1024, 128, dtype=F32), like(32, 128)] + [like(1056, 128)] * 3,
        r_all, swap(own), p1, p3, pieces,
    )
    got = [hop(sent[k - 1], second, k) for k in (2, 1, 3)]
    rest, pieces, *sent = in_vmem(
        "plane_sum", plane_sum, [like(256, 128, dtype=F32), like(128, 128)] + [like(384, 128)] * 3,
        own, piece, *got,
    )
    got = [hop(sent[k - 1], first, k) for k in (2, 1, 3)]
    own = in_vmem("extra_half", extra_half, [like(264, 128, dtype=F32)], pieces, *got)[0]
    other = swap(own)
    grad_features = in_vmem(
        "finish", finish, [like(128, 256, dtype=F32)], rest, *got, weight, last=True
    )[0]
    grad_weight, grad_bias = extras(own, other)
    return activation, grad_weight, grad_bias[0], grad_features


def extras(own, other):
    vmem = pl.BlockSpec(memory_space=pltpu.VMEM)

    def body(own, other, dw, db):
        extra_both(lax.axis_index(AXIS) & 1, own, other, dw, db)

    return pl.pallas_call(
        body,
        out_shape=(like(256, 256, dtype=F32), like(1, 256, dtype=F32)),
        in_specs=[vmem] * 2,
        out_specs=(vmem,) * 2,
        compiler_params=pltpu.CompilerParams(vmem_limit_bytes=4 * 1024 * 1024),
        name="extras",
    )(own, other)


def solution(mesh):
    in_specs = (
        P("rows", None),
        P("rows", None, None, None),
        P("rows", None),
        P("rows"),
        P(),
        P(),
        P("rows", None),
    )
    out_specs = (P("rows", None), P(), P(), P("rows", None))
    return jax.shard_map(
        on_device, mesh=mesh, in_specs=in_specs, out_specs=out_specs, check_vma=False
    )
```
